256 devices in a mesh: ctx: 32 (over x, z_lo, y), head: 8 (over z_hi, core).
Axes of the slice: x: 4, y: 4, z: 8 (z_hi: 4, z_lo: 2; z = z_hi * 2 + z_lo), core: 2. Of those that a mesh axis runs over, the one named last changes fastest.
Arguments:
- queries: bfloat16 [8192, 56, 128], P('ctx', 'head'), may hold values from -6 to 6
- keys: bfloat16 [8192, 8, 128], P('ctx', 'head'), may hold values from -6 to 6
- values: bfloat16 [8192, 8, 128], P('ctx', 'head'), may hold values from -6 to 6
- out_weight: bfloat16 [7168, 3584], P('head'), may hold values from -0.0625 to 0.0625
- segment_info: int32 [64, 3], replicated, may hold values from 0 to 8192, as said below
- block_order: int32 [64], replicated, may hold values from 0 to 63, each once
Outputs:
- projected: bfloat16 [8192, 3584], P(('ctx', 'head'))
The draws below stay inside these ranges and needn't reach their ends.
Inputs may be any that keep to these rules, and one draw needn't show every extreme that they name: `segment_info`: segments are runs of 1 to 4 whole prompt blocks that cover the prompt in order; all blocks of a segment have equal rows; the first segment is causal.
All inputs are finite; a program needn't handle non-finite values.
Results may differ from the reference program's by a relative error of at most 0.02.
Values may be sent and summed in bfloat16 or wider, within the bound.
No kernel may reach another device: no remote copies, remote signals or barrier semaphores. Data moves between devices by JAX's collectives and lax.ppermute only.
A program may use at most 64 MiB of HBM per device.

```python
import jax
import jax.numpy as jnp
from jax import lax

HQ = 56
KVH = 8
HD = 128
DW = 3584
BLK = 128
SEG_MOST = 4
SEQ = 8192
BLOCKS = 64


def draw_queries(key, part):
    key = jax.random.fold_in(key, 1)
    key_main = jax.random.fold_in(key, 0)
    normal_part = jnp.clip(1.6 * jax.random.normal(key_main, (SEQ, HQ, HD), jnp.float32), -6.0, 6.0)
    return normal_part.astype(jnp.bfloat16)


def draw_keys(key, part):
    key = jax.random.fold_in(key, 2)
    key_main = jax.random.fold_in(key, 0)
    normal_part = jnp.clip(1.6 * jax.random.normal(key_main, (SEQ, KVH, HD), jnp.float32), -6.0, 6.0)
    return normal_part.astype(jnp.bfloat16)


def draw_segment_info(key, part):
    key = jax.random.fold_in(key, 11)
    key_length, key_kind = jax.random.split(key)
    seg_lengths = jax.random.randint(key_length, (BLOCKS,), 1, SEG_MOST + 1).astype(jnp.int32)
    seg_lengths = seg_lengths.at[1].set(SEG_MOST)
    seg_ends = jnp.cumsum(seg_lengths).astype(jnp.int32)
    seg_starts = seg_ends - seg_lengths
    block_ids = jnp.arange(BLOCKS, dtype=jnp.int32)
    seg_ids = jnp.sum((seg_ends[None, :] <= block_ids[:, None]).astype(jnp.int32), axis=1)
    first_block = jnp.take(seg_starts, seg_ids)
    end_block = jnp.minimum(jnp.take(seg_ends, seg_ids), BLOCKS)
    seg_kinds = jax.random.randint(key_kind, (BLOCKS,), 0, 2).astype(jnp.int32).at[0].set(0)
    kind_column = jnp.take(seg_kinds, seg_ids)
    return jnp.stack([first_block * BLK, end_block * BLK, kind_column], axis=1).astype(jnp.int32)


def levels(own_key, extent, cuts, smallest, top_value):
    loudness = 1.0
    for dim, shards_of in cuts:
        steps = jax.random.uniform(jax.random.fold_in(jax.random.fold_in(own_key, 6), dim), (shards_of,), jnp.float32, smallest / len(cuts), top_value / len(cuts))
        loudness = loudness * jnp.repeat(jnp.exp(steps), extent[dim] // shards_of).reshape((-1,) + (1,) * (len(extent) - 1 - dim))
    return loudness


def noise(own_key, extent, spread, reach, pieces=(), kind=jnp.bfloat16):
    level = levels(own_key, extent, pieces, -0.22, 0.18) if pieces else 1.0
    entries = jax.random.normal(own_key, extent, jnp.float32) * spread * level
    return jnp.minimum(jnp.maximum(entries, -reach), reach).astype(kind)


def setup_inputs(seed: int = 0) -> dict:
    key_of = jax.random.split(jax.random.key(seed), 7)
    return {
        "queries": draw_queries(jax.random.fold_in(key_of[6], 71), 0),
        "keys": draw_keys(jax.random.fold_in(key_of[6], 71), 0),
        "values": noise(key_of[2], (SEQ, KVH, HD), 1.0, 6.0, ((0, 32), (1, 8))),
        "out_weight": noise(key_of[3], (HQ * HD, DW), (HQ * HD) ** -0.5, 0.0625, ((0, 8),)),
        "segment_info": draw_segment_info(jax.random.fold_in(key_of[6], 71), 0),
        "block_order": jax.random.permutation(key_of[5], BLOCKS).astype(jnp.int32),
    }


def reference(queries, keys, values, out_weight, segment_info, block_order):
    seq_rows = queries.shape[0]
    group_size = HQ // KVH
    score_scale = HD ** -0.5
    row_ids = jnp.arange(seq_rows, dtype=jnp.int32)
    block_ids = jnp.take(block_order, row_ids // BLK)
    positions = block_ids * BLK + row_ids % BLK
    row_info = jnp.take(segment_info, block_ids, axis=0)
    keys_wide = keys.astype(jnp.float32)
    values_wide = values.astype(jnp.float32)

    def one_tile(tile_index):
        first_row = (tile_index * BLK).astype(jnp.int32)
        query_tile = lax.dynamic_slice_in_dim(queries, first_row, BLK, 0).astype(jnp.float32)
        query_tile = query_tile.reshape(BLK, KVH, group_size, HD)
        query_pos = lax.dynamic_slice_in_dim(positions, first_row, BLK, 0)
        query_info = lax.dynamic_slice_in_dim(row_info, first_row, BLK, 0)
        scores = jnp.einsum("qgjd,kgd->qgjk", query_tile, keys_wide) * score_scale
        before = positions[None, :] <= query_pos[:, None]
        inside = (query_info[:, 2:3] == 1) & (positions[None, :] >= query_info[:, 0:1]) & (positions[None, :] < query_info[:, 1:2])
        allowed = (before | inside)[:, None, None, :]
        scores = jnp.where(allowed, scores, -jnp.inf)
        row_max = jnp.max(scores, axis=-1, keepdims=True)
        weights = jnp.where(allowed, jnp.exp(scores - row_max), 0.0)
        row_sum = jnp.sum(weights, axis=-1)
        weights_low = lax.optimization_barrier(weights.astype(jnp.bfloat16)).astype(jnp.float32)
        outputs = jnp.einsum("qgjk,kgd->qgjd", weights_low, values_wide) / row_sum[..., None]
        return outputs.reshape(BLK, HQ, HD).astype(jnp.bfloat16)

    attended = lax.map(one_tile, jnp.arange(seq_rows // BLK, dtype=jnp.int32))
    attended = attended.reshape(seq_rows, HQ * HD)
    return jnp.dot(attended, out_weight, preferred_element_type=jnp.float32).astype(jnp.bfloat16)
```

```python
import functools
import math

import jax
import jax.numpy as jnp
from jax import lax
from jax.experimental import pallas as pl
from jax.experimental.pallas import tpu as pltpu
from jax.sharding import Mesh, PartitionSpec as P

BLK = 128
HD = 128
GROUP = 7
ROWS = 256
FEATS = GROUP * HD
BLOCKS = 64
CHUNK = 8
MINUS = -1e30
SIZES = {"x": 4, "zl": 2, "y": 4, "zh": 4, "core": 2}
AXES = tuple(SIZES)
CTX = ("x", "zl", "y")
HEAD = ("zh", "core")
OFFSETS = (0, -1, 1, 2)


def shift(value, axis, step):
    size = SIZES[axis]
    return lax.ppermute(value, axis, [((i + step) % size, i) for i in range(size)])


def ring_index(there, here):
    off = (there - here) & 3
    return jnp.where(off == 0, 0, jnp.where(off == 3, 1, jnp.where(off == 1, 2, 3)))


def attend_kernel(order_ref, info_ref, where_ref, q_ref, *refs):
    parts = refs[:8]
    w_hbm, keep_ref, send_ref = refs[8:11]
    slot_ref, kv_ref, w_ref, qs_ref, m_ref, l_ref, acc_ref, att_ref, kv_sem, w_sem = refs[11:]
    w_copy = pltpu.make_async_copy(w_hbm, w_ref, w_sem)
    part_rows = parts[0].shape[0]
    copies = [
        pltpu.make_async_copy(part, kv_ref.at[pl.ds(i * part_rows, part_rows)], kv_sem.at[i])
        for i, part in enumerate(parts)
    ]
    for copy in copies:
        copy.start()
    w_copy.start()
    my_x, my_zl, my_y, my_zh, my_core = (where_ref[i] for i in range(5))
    first_block = ((my_x * 2 + my_zl) * 4 + my_y) * 2

    def place(block, _):
        ctx = block >> 1
        x_part = ring_index(ctx >> 3, my_x)
        y_part = ring_index(ctx & 3, my_y)
        even = (block & 1) == 0
        outer = jnp.where(even, x_part, 4 + y_part)
        inner = jnp.where(even, y_part, x_part)
        slot_ref[order_ref[block]] = (outer * 4 + inner) * 2 + (((ctx >> 2) & 1) ^ my_zl)
        return 0

    lax.fori_loop(0, BLOCKS, place, 0)
    scale = math.log2(math.e) / math.sqrt(HD)
    rows = GROUP * BLK
    wide = CHUNK * BLK
    for copy in copies:
        copy.wait()
    for t in range(2):
        block = order_ref[first_block + t]
        last = info_ref[block * 3 + 1]
        kind = info_ref[block * 3 + 2]
        limit = jnp.where(kind == 1, last, (block + 1) * BLK)
        for h in range(GROUP):
            scaled = q_ref[h, t * BLK : (t + 1) * BLK, :].astype(jnp.float32) * scale
            high = scaled.astype(jnp.bfloat16)
            qs_ref[h * BLK : (h + 1) * BLK, 0:HD] = high
            qs_ref[h * BLK : (h + 1) * BLK, HD:] = (scaled - high.astype(jnp.float32)).astype(jnp.bfloat16)
        m_ref[...] = jnp.full_like(m_ref, MINUS)
        l_ref[...] = jnp.zeros_like(l_ref)
        acc_ref[...] = jnp.zeros_like(acc_ref)

        def step(chunk, masked):
            key_list, value_list = [], []
            for j in range(CHUNK):
                slot = slot_ref[jnp.minimum(chunk * CHUNK + j, BLOCKS - 1)]
                start = pl.multiple_of(slot * (2 * BLK), 2 * BLK)
                key_list.append(kv_ref[pl.ds(start, BLK), :])
                value_list.append(kv_ref[pl.ds(start + BLK, BLK), :])
            key_tile = jnp.concatenate(key_list, axis=0)
            value_tile = jnp.concatenate(value_list, axis=0)
            twice = jnp.concatenate([key_tile, key_tile], axis=1)
            s = lax.dot_general(
                qs_ref[...], twice, (((1,), (1,)), ((), ())), preferred_element_type=jnp.float32
            )
            if masked:
                col = chunk * wide + lax.broadcasted_iota(jnp.int32, (rows, wide), 1)
                row = lax.broadcasted_iota(jnp.int32, (rows, wide), 0) & (BLK - 1)
                most = jnp.where(kind == 1, last - 1, block * BLK + row)
                s = jnp.where(col <= most, s, MINUS)
            m_old = m_ref[...]
            m_new = jnp.maximum(m_old, jnp.max(s, axis=1, keepdims=True))
            p = jnp.exp2(s - jnp.concatenate([m_new] * CHUNK, axis=1))
            fade = jnp.exp2(m_old - m_new)
            l_ref[...] = l_ref[...] * fade + sum(p[:, i * BLK : (i + 1) * BLK] for i in range(CHUNK))
            m_ref[...] = m_new
            acc_ref[...] = acc_ref[...] * fade + jnp.dot(
                p.astype(jnp.bfloat16), value_tile, preferred_element_type=jnp.float32
            )

        chunks = lax.div(limit + (wide - 1), wide)

        def full_step(chunk, _):
            step(chunk, False)
            return 0

        lax.fori_loop(0, chunks - 1, full_step, 0)
        step(chunks - 1, True)
        for h in range(GROUP):
            part = slice(h * BLK, (h + 1) * BLK)
            total = jnp.sum(l_ref[part, :], axis=1, keepdims=True)
            att_ref[t * BLK : (t + 1) * BLK, h * HD : (h + 1) * HD] = (acc_ref[part, :] / total).astype(jnp.bfloat16)
    w_copy.wait()
    out_cols = w_ref.shape[1]
    tile = 512

    def project(index, _):
        cols = pl.ds(pl.multiple_of(index * tile, tile), tile)
        res = jnp.dot(att_ref[...], w_ref[:, cols], preferred_element_type=jnp.float32).astype(jnp.bfloat16)
        for z in range(4):
            to = (z - my_zh) & 3
            zero, one = res[z * 64 : z * 64 + 32, :], res[z * 64 + 32 : z * 64 + 64, :]
            keep_ref[to, :, cols] = jnp.where(my_core == 0, zero, one)
            send_ref[to, :, cols] = jnp.where(my_core == 0, one, zero)
        return 0

    lax.fori_loop(0, out_cols // tile, project, 0)


def attend(order, info, where, q, parts, w):
    part_rows = parts[0].shape[0]
    out_cols = w.shape[1]
    rows = GROUP * BLK
    piece = jax.ShapeDtypeStruct((4, 32, out_cols), jnp.bfloat16)
    smem = pl.BlockSpec(memory_space=pltpu.SMEM)
    vmem = pl.BlockSpec(memory_space=pltpu.VMEM)
    anywhere = pl.BlockSpec(memory_space=pl.ANY)
    return pl.pallas_call(
        attend_kernel,
        out_shape=(piece, piece),
        in_specs=[smem, smem, smem, vmem] + [anywhere] * 9,
        out_specs=(vmem, vmem),
        scratch_shapes=[
            pltpu.SMEM((BLOCKS,), jnp.int32),
            pltpu.VMEM((8 * part_rows, HD), jnp.bfloat16),
            pltpu.VMEM(w.shape, jnp.bfloat16),
            pltpu.VMEM((rows, 2 * HD), jnp.bfloat16),
            pltpu.VMEM((rows, BLK), jnp.float32),
            pltpu.VMEM((rows, BLK), jnp.float32),
            pltpu.VMEM((rows, HD), jnp.float32),
            pltpu.VMEM((ROWS, FEATS), jnp.bfloat16),
            pltpu.SemaphoreType.DMA((8,)),
            pltpu.SemaphoreType.DMA,
        ],
        compiler_params=pltpu.CompilerParams(vmem_limit_bytes=48 * 1024 * 1024),
        cost_estimate=pl.CostEstimate(flops=9_000_000_000, bytes_accessed=14_000_000, transcendentals=8_000_000),
        name="attend",
    )(order, info, where, q, *parts, w)


def body(queries, keys, values, out_weight, segment_info, block_order):
    where = jnp.stack([lax.axis_index(axis) for axis in AXES]).astype(jnp.int32)
    k, v = keys[:, 0, :], values[:, 0, :]
    mine = jnp.concatenate([k[:BLK], v[:BLK], k[BLK:], v[BLK:]], axis=0)
    pair = shift(mine, "zl", 1)
    first = jnp.concatenate([mine[: 2 * BLK], pair[: 2 * BLK]], axis=0)
    second = jnp.concatenate([mine[2 * BLK :], pair[2 * BLK :]], axis=0)
    first = jnp.concatenate([first] + [shift(first, "y", o) for o in OFFSETS[1:]], axis=0)
    second = jnp.concatenate([second] + [shift(second, "x", o) for o in OFFSETS[1:]], axis=0)
    parts = [first] + [shift(first, "x", o) for o in OFFSETS[1:]]
    parts += [second] + [shift(second, "y", o) for o in OFFSETS[1:]]
    q = jnp.transpose(queries, (1, 0, 2))
    keep, send = attend(block_order, segment_info.reshape(-1), where, q, parts, out_weight)
    pieces = keep.astype(jnp.float32) + shift(send, "core", 1).astype(jnp.float32)
    low = pieces.astype(jnp.bfloat16)
    total = pieces[0]
    for j in (1, 3, 2):
        total = total + shift(low[j], "zh", -j).astype(jnp.float32)
    return total.astype(jnp.bfloat16)


def solution(mesh):
    fine = Mesh(mesh.devices.reshape(tuple(SIZES.values())), AXES)
    placed = (
        P(CTX, HEAD, None),
        P(CTX, HEAD, None),
        P(CTX, HEAD, None),
        P(HEAD, None),
        P(),
        P(),
    )
    return jax.shard_map(body, mesh=fine, in_specs=placed, out_specs=P(AXES, None), check_vma=False)
```

```python
import functools
import math

import jax
import jax.numpy as jnp
from jax import lax
from jax.experimental import pallas as pl
from jax.experimental.pallas import tpu as pltpu
from jax.sharding import Mesh, PartitionSpec as P

BLK = 128
HD = 128
GROUP = 7
ROWS = 256
FEATS = GROUP * HD
BLOCKS = 64
CHUNK = 16
MINUS = -1e30
SIZES = {"x": 4, "zl": 2, "y": 4, "zh": 4, "core": 2}
AXES = tuple(SIZES)
CTX = ("x", "zl", "y")
HEAD = ("zh", "core")
OFFSETS = (0, -1, 1, 2)
SMEM = pl.BlockSpec(memory_space=pltpu.SMEM)
VMEM = pl.BlockSpec(memory_space=pltpu.VMEM)
ANYWHERE = pl.BlockSpec(memory_space=pl.ANY)


def shift(value, axis, step):
    size = SIZES[axis]
    return lax.ppermute(value, axis, [((i + step) % size, i) for i in range(size)])


def ring_index(there, here):
    off = (there - here) & 3
    return jnp.where(off == 0, 0, jnp.where(off == 3, 1, jnp.where(off == 1, 2, 3)))


def table_kernel(order_ref, where_ref, table_ref, inv_ref):
    my_x, my_zl, my_y = where_ref[0], where_ref[1], where_ref[2]

    def invert(block, _):
        inv_ref[order_ref[block]] = block
        table_ref[block] = 0
        table_ref[BLOCKS + block] = BLOCKS
        return 0

    lax.fori_loop(0, BLOCKS, invert, 0)

    def place(position, count):
        block = inv_ref[position]
        ctx = block >> 1
        x_part = ring_index(ctx >> 3, my_x)
        y_part = ring_index(ctx & 3, my_y)
        even = (block & 1) == 0
        here = ((ctx >> 2) & 1) == my_zl

        @pl.when(here)
        def _():
            table_ref[count] = jnp.where(even, x_part * 4 + y_part, 16 + y_part * 4 + x_part)
            table_ref[BLOCKS + count] = position

        count = count + here.astype(jnp.int32)
        table_ref[2 * BLOCKS + position] = count
        return count

    lax.fori_loop(0, BLOCKS, place, jnp.int32(0))


def make_table(order, where):
    return pl.pallas_call(
        table_kernel,
        out_shape=jax.ShapeDtypeStruct((3 * BLOCKS,), jnp.int32),
        in_specs=[SMEM, SMEM],
        out_specs=SMEM,
        scratch_shapes=[pltpu.SMEM((BLOCKS,), jnp.int32)],
        name="table",
    )(order, where)


def attend_kernel(flip, order_ref, info_ref, where_ref, table_ref, q_ref, *refs):
    parts = refs[:8]
    out_ref, kv_ref, qs_ref, m_ref, l_ref, acc_ref, kv_sem = refs[8:]
    part_rows = parts[0].shape[0]
    copies = [
        pltpu.make_async_copy(part, kv_ref.at[pl.ds(i * part_rows, part_rows)], kv_sem.at[i])
        for i, part in enumerate(parts)
    ]
    for copy in copies:
        copy.start()
    my_x, my_zl, my_y = where_ref[0], where_ref[1], where_ref[2]
    first_block = ((my_x * 2 + (my_zl ^ flip)) * 4 + my_y) * 2
    scale = math.log2(math.e) / math.sqrt(HD)
    rows = GROUP * BLK
    for copy in copies:
        copy.wait()

    def one_block(t, _):
        block = order_ref[first_block + t]
        last = info_ref[block * 3 + 1]
        kind = info_ref[block * 3 + 2]
        most_block = jnp.where(kind == 1, lax.div(last, BLK) - 1, block)
        count = table_ref[2 * BLOCKS + most_block]
        q_rows = pl.ds(pl.multiple_of(t * BLK, BLK), BLK)
        for h in range(GROUP):
            scaled = q_ref[h, q_rows, :].astype(jnp.float32) * scale
            high = scaled.astype(jnp.bfloat16)
            qs_ref[h * BLK : (h + 1) * BLK, 0:HD] = high
            qs_ref[h * BLK : (h + 1) * BLK, HD:] = (scaled - high.astype(jnp.float32)).astype(jnp.bfloat16)
        m_ref[...] = jnp.full_like(m_ref, MINUS)
        l_ref[...] = jnp.zeros_like(l_ref)
        acc_ref[...] = jnp.zeros_like(acc_ref)

        def step(begin, size, masked):
            key_list, value_list = [], []
            for j in range(size):
                start = pl.multiple_of(table_ref[begin + j] * (2 * BLK), 2 * BLK)
                key_list.append(kv_ref[pl.ds(start, BLK), :])
                value_list.append(kv_ref[pl.ds(start + BLK, BLK), :])
            key_tile = jnp.concatenate(key_list, axis=0)
            value_tile = jnp.concatenate(value_list, axis=0)
            twice = jnp.concatenate([key_tile, key_tile], axis=1)
            s = lax.dot_general(
                qs_ref[...], twice, (((1,), (1,)), ((), ())), preferred_element_type=jnp.float32
            )
            if masked:
                lane = lax.broadcasted_iota(jnp.int32, (rows, BLK), 1)
                row = lax.broadcasted_iota(jnp.int32, (rows, BLK), 0) & (BLK - 1)
                most = jnp.where(kind == 1, last - 1, block * BLK + row) - lane
                s = jnp.concatenate(
                    [
                        jnp.where(
                            table_ref[BLOCKS + begin + j] * BLK <= most, s[:, j * BLK : (j + 1) * BLK], MINUS
                        )
                        for j in range(size)
                    ],
                    axis=1,
                )
            m_old = m_ref[...]
            m_new = jnp.maximum(m_old, jnp.max(s, axis=1, keepdims=True))
            p = jnp.exp2(s - jnp.concatenate([m_new] * size, axis=1))
            fade = jnp.exp2(m_old - m_new)
            l_ref[...] = l_ref[...] * fade + sum(p[:, i * BLK : (i + 1) * BLK] for i in range(size))
            m_ref[...] = m_new
            acc_ref[...] = acc_ref[...] * fade + jnp.dot(
                p.astype(jnp.bfloat16), value_tile, preferred_element_type=jnp.float32
            )

        full = lax.div(jnp.maximum(count - 1, 0), CHUNK)

        def full_step(chunk, _):
            step(chunk * CHUNK, CHUNK, False)
            return 0

        lax.fori_loop(0, full, full_step, 0)
        rest = count - full * CHUNK
        for size in (4, 8, 12, 16):

            @pl.when((rest > size - 4) & (rest <= size))
            def _(size=size):
                step(full * CHUNK, size, True)

        lane = lax.broadcasted_iota(jnp.int32, (BLK, BLK), 1)
        stats = jnp.zeros((BLK, BLK), jnp.float32)
        for h in range(GROUP):
            part = slice(h * BLK, (h + 1) * BLK)
            total = jnp.sum(l_ref[part, :], axis=1, keepdims=True)
            safe = jnp.where(total > 0, total, 1.0)
            out_ref[q_rows, h * HD : (h + 1) * HD] = (acc_ref[part, :] / safe).astype(jnp.bfloat16)
            level = m_ref[part, :] + jnp.log2(safe)
            high = level.astype(jnp.bfloat16).astype(jnp.float32)
            middle = (level - high).astype(jnp.bfloat16).astype(jnp.float32)
            stats = jnp.where(lane == h, high, stats)
            stats = jnp.where(lane == 8 + h, middle, stats)
            stats = jnp.where(lane == 16 + h, level - high - middle, stats)
        out_ref[q_rows, FEATS:] = stats.astype(jnp.bfloat16)
        return 0

    lax.fori_loop(0, 2, one_block, 0)


def attend(flip, order, info, where, table, q, parts):
    part_rows = parts[0].shape[0]
    rows = GROUP * BLK
    return pl.pallas_call(
        functools.partial(attend_kernel, flip),
        out_shape=jax.ShapeDtypeStruct((ROWS, FEATS + BLK), jnp.bfloat16),
        in_specs=[SMEM, SMEM, SMEM, SMEM, VMEM] + [ANYWHERE] * 8,
        out_specs=VMEM,
        scratch_shapes=[
            pltpu.VMEM((8 * part_rows, HD), jnp.bfloat16),
            pltpu.VMEM((rows, 2 * HD), jnp.bfloat16),
            pltpu.VMEM((rows, BLK), jnp.float32),
            pltpu.VMEM((rows, BLK), jnp.float32),
            pltpu.VMEM((rows, HD), jnp.float32),
            pltpu.SemaphoreType.DMA((8,)),
        ],
        compiler_params=pltpu.CompilerParams(vmem_limit_bytes=40 * 1024 * 1024),
        cost_estimate=pl.CostEstimate(flops=4_000_000_000, bytes_accessed=3_000_000, transcendentals=4_000_000),
        name="attend",
    )(order, info, where, table, q, *parts)


def project_kernel(where_ref, a_ref, b_ref, w_ref, keep_ref, send_ref, att_ref):
    my_zh, my_core = where_ref[3], where_ref[4]

    @pl.when(pl.program_id(0) == 0)
    def _():
        stats_a = a_ref[:, FEATS:].astype(jnp.float32)
        stats_b = b_ref[:, FEATS:].astype(jnp.float32)
        for h in range(GROUP):

            def level(stats):
                return stats[:, h : h + 1] + stats[:, 8 + h : 9 + h] + stats[:, 16 + h : 17 + h]

            weight_a = 1.0 / (1.0 + jnp.exp2(level(stats_b) - level(stats_a)))
            cols = slice(h * HD, (h + 1) * HD)
            a, b = a_ref[:, cols].astype(jnp.float32), b_ref[:, cols].astype(jnp.float32)
            att_ref[:, cols] = (b + (a - b) * weight_a).astype(jnp.bfloat16)

    res = jnp.dot(att_ref[...], w_ref[...], preferred_element_type=jnp.float32).astype(jnp.bfloat16)
    for z in range(4):
        to = (z - my_zh) & 3
        zero, one = res[z * 64 : z * 64 + 32, :], res[z * 64 + 32 : z * 64 + 64, :]
        keep_ref[to] = jnp.where(my_core == 0, zero, one)
        send_ref[to] = jnp.where(my_core == 0, one, zero)


def project(where, a, b, w):
    out_cols = w.shape[1]
    tile = 512
    piece = jax.ShapeDtypeStruct((4, 32, out_cols), jnp.bfloat16)
    out_spec = pl.BlockSpec((4, 32, tile), lambda i: (0, 0, i))
    return pl.pallas_call(
        project_kernel,
        grid=(out_cols // tile,),
        out_shape=(piece, piece),
        in_specs=[
            SMEM,
            pl.BlockSpec(a.shape, lambda i: (0, 0)),
            pl.BlockSpec(b.shape, lambda i: (0, 0)),
            pl.BlockSpec((w.shape[0], tile), lambda i: (0, i)),
        ],
        out_specs=(out_spec, out_spec),
        scratch_shapes=[pltpu.VMEM((ROWS, FEATS), jnp.bfloat16)],
        compiler_params=pltpu.CompilerParams(vmem_limit_bytes=24 * 1024 * 1024),
        cost_estimate=pl.CostEstimate(flops=1_640_000_000, bytes_accessed=9_000_000, transcendentals=1792),
        name="project",
    )(where, a, b, w)


def body(queries, keys, values, out_weight, segment_info, block_order):
    where = jnp.stack([lax.axis_index(axis) for axis in AXES]).astype(jnp.int32)
    info = segment_info.reshape(-1)
    k, v = keys[:, 0, :], values[:, 0, :]
    q = jnp.transpose(queries, (1, 0, 2))
    first = jnp.concatenate([k[:BLK], v[:BLK]], axis=0)
    second = jnp.concatenate([k[BLK:], v[BLK:]], axis=0)
    first = jnp.concatenate([first] + [shift(first, "y", o) for o in OFFSETS[1:]], axis=0)
    second = jnp.concatenate([second] + [shift(second, "x", o) for o in OFFSETS[1:]], axis=0)
    parts = [first] + [shift(first, "x", o) for o in OFFSETS[1:]]
    parts += [second] + [shift(second, "y", o) for o in OFFSETS[1:]]
    other_q = shift(q, "zl", 1)
    table = make_table(block_order, where)
    other = attend(1, block_order, info, where, table, other_q, parts)
    back = shift(other, "zl", 1)
    own = attend(0, block_order, info, where, table, q, parts)
    keep, send = project(where, own, back, out_weight)
    pieces = keep.astype(jnp.float32) + shift(send, "core", 1).astype(jnp.float32)
    low = pieces.astype(jnp.bfloat16)
    total = pieces[0]
    for j in (1, 3, 2):
        total = total + shift(low[j], "zh", -j).astype(jnp.float32)
    return total.astype(jnp.bfloat16)


def solution(mesh):
    fine = Mesh(mesh.devices.reshape(tuple(SIZES.values())), AXES)
    placed = (
        P(CTX, HEAD, None),
        P(CTX, HEAD, None),
        P(CTX, HEAD, None),
        P(HEAD, None),
        P(),
        P(),
    )
    return jax.shard_map(body, mesh=fine, in_specs=placed, out_specs=P(AXES, None), check_vma=False)
```

```python
import functools
import math

import jax
import jax.numpy as jnp
from jax import lax
from jax.experimental import pallas as pl
from jax.experimental.pallas import tpu as pltpu
from jax.sharding import Mesh, PartitionSpec as P

BLK = 128
HD = 128
GROUP = 7
ROWS = 256
FEATS = GROUP * HD
BLOCKS = 64
CHUNK = 16
LIST = 48
QUERY_AT = 3 * LIST
HEAD_AT = QUERY_AT + 16
TABLE = 256
MINUS = -1e30
SIZES = {"x": 4, "zl": 2, "y": 4, "zh": 4, "core": 2}
AXES = tuple(SIZES)
CTX = ("x", "zl", "y")
HEAD = ("zh", "core")
OFFSETS = (0, 1, -1, 2)
PLACES = (0, 4, 5, 1, 6, 2, 7, 3)
SMEM = pl.BlockSpec(memory_space=pltpu.SMEM)
VMEM = pl.BlockSpec(memory_space=pltpu.VMEM)
ANYWHERE = pl.BlockSpec(memory_space=pl.ANY)


def shift(value, axis, step):
    size = SIZES[axis]
    return lax.ppermute(value, axis, [((i + step) % size, i) for i in range(size)])


def table_kernel(order_ref, info_ref, table_ref, inv_ref):
    my_x, my_zl, my_y = (lax.axis_index(axis) for axis in CTX)

    def invert(block, _):
        inv_ref[order_ref[block]] = block
        return 0

    lax.fori_loop(0, BLOCKS, invert, 0)
    table_ref[HEAD_AT] = lax.axis_index("zh")
    table_ref[HEAD_AT + 1] = lax.axis_index("core")
    ends = []
    for i in range(4):
        pair_zl = my_zl ^ 1 if i < 2 else my_zl
        block = order_ref[((my_x * 2 + pair_zl) * 4 + my_y) * 2 + i % 2]
        last, kind = info_ref[1, block], info_ref[2, block]
        at = QUERY_AT + 4 * i
        table_ref[at], table_ref[at + 1], table_ref[at + 2] = block, kind, last
        ends.append(jnp.where(kind == 1, lax.div(last, BLK) - 1, block))

    def place(position, carry):
        count, seen = carry[0], carry[1:]
        block = inv_ref[position]
        ctx = block >> 1
        x_off, y_off = ((ctx >> 3) - my_x) & 3, ((ctx & 3) - my_y) & 3
        x_part, y_part = (x_off ^ (x_off >> 1)), (y_off ^ (y_off >> 1))
        here = ((ctx >> 2) & 1) == my_zl
        table_ref[count] = (x_part * 4 + y_part) * 2 + (block & 1)
        table_ref[LIST + count] = (y_part * 4 + x_part) * 2 + (block & 1)
        table_ref[2 * LIST + count] = position
        count = count + here.astype(jnp.int32)
        return (count,) + tuple(jnp.where(position == end, count, s) for end, s in zip(ends, seen))

    done = lax.fori_loop(0, BLOCKS, place, (jnp.int32(0),) * 5)
    for i in range(4):
        table_ref[QUERY_AT + 4 * i + 3] = done[1 + i]
    for i in range(BLOCKS // 2, LIST):
        table_ref[i] = 0
        table_ref[LIST + i] = 0
        table_ref[2 * LIST + i] = BLOCKS


def make_table(order, info):
    return pl.pallas_call(
        table_kernel,
        out_shape=jax.ShapeDtypeStruct((TABLE,), jnp.int32),
        in_specs=[SMEM, SMEM],
        out_specs=SMEM,
        scratch_shapes=[pltpu.SMEM((BLOCKS,), jnp.int32)],
        cost_estimate=pl.CostEstimate(flops=2_000_000_000, bytes_accessed=1000, transcendentals=0),
        name="table",
    )(order, info)


def attend_kernel(side, table_hbm, q_hbm, *refs):
    parts = refs[:8]
    out_hbm, table_ref, q_ref, out_ref, kv_ref, qs_ref, m_ref, l_ref, acc_ref, kv_sem, in_sem, out_sem = refs[8:]
    part_rows = parts[0].shape[0]
    half = 4 * part_rows
    table_copy = pltpu.make_async_copy(table_hbm, table_ref, in_sem.at[0])
    q_copy = pltpu.make_async_copy(q_hbm, q_ref, in_sem.at[1])
    copies = [
        pltpu.make_async_copy(part, kv_ref.at[pl.ds(i * part_rows, part_rows)], kv_sem.at[i])
        for i, part in zip(PLACES, parts)
    ]
    out_copies = [
        pltpu.make_async_copy(
            out_ref.at[pl.ds(t * BLK, BLK)], out_hbm.at[pl.ds(t * BLK, BLK)], out_sem.at[t]
        )
        for t in range(2)
    ]
    table_copy.start()
    q_copy.start()
    for copy in copies:
        copy.start()
    scale = math.log2(math.e) / math.sqrt(HD)
    rows = GROUP * BLK
    q_copy.wait()
    table_copy.wait()
    for copy in copies:
        copy.wait()

    def one_block(t, _):
        at = QUERY_AT + 4 * (2 * side + t)
        block, kind, last, count = table_ref[at], table_ref[at + 1], table_ref[at + 2], table_ref[at + 3]
        q_rows = pl.ds(pl.multiple_of(t * BLK, BLK), BLK)
        for h in range(GROUP):
            scaled = q_ref[h, q_rows, :].astype(jnp.float32) * scale
            high = scaled.astype(jnp.bfloat16)
            qs_ref[h * BLK : (h + 1) * BLK, 0:HD] = high
            qs_ref[h * BLK : (h + 1) * BLK, HD:] = (scaled - high.astype(jnp.float32)).astype(jnp.bfloat16)
        m_ref[...] = jnp.full_like(m_ref, MINUS)
        l_ref[...] = jnp.zeros_like(l_ref)
        acc_ref[...] = jnp.zeros_like(acc_ref)

        def step(begin, size, masked):
            key_list, value_list = [], []
            for j in range(size):
                key_at = pl.multiple_of(table_ref[begin + j] * BLK, BLK)
                value_at = pl.multiple_of(table_ref[LIST + begin + j] * BLK, BLK)
                key_list.append(kv_ref[pl.ds(key_at, BLK), :])
                value_list.append(kv_ref[pl.ds(value_at + half, BLK), :])
            key_tile = jnp.concatenate(key_list, axis=0)
            value_tile = jnp.concatenate(value_list, axis=0)
            twice = jnp.concatenate([key_tile, key_tile], axis=1)
            s = lax.dot_general(
                qs_ref[...], twice, (((1,), (1,)), ((), ())), preferred_element_type=jnp.float32
            )
            if masked:
                lane = lax.broadcasted_iota(jnp.int32, (rows, BLK), 1)
                row = lax.broadcasted_iota(jnp.int32, (rows, BLK), 0) & (BLK - 1)
                most = jnp.where(kind == 1, last - 1, block * BLK + row) - lane
                s = jnp.concatenate(
                    [
                        jnp.where(
                            table_ref[2 * LIST + begin + j] * BLK <= most, s[:, j * BLK : (j + 1) * BLK], MINUS
                        )
                        for j in range(size)
                    ],
                    axis=1,
                )
            m_old = m_ref[...]
            m_new = jnp.maximum(m_old, jnp.max(s, axis=1, keepdims=True))
            p = jnp.exp2(s - jnp.concatenate([m_new] * size, axis=1))
            fade = jnp.exp2(m_old - m_new)
            l_ref[...] = l_ref[...] * fade + sum(p[:, i * BLK : (i + 1) * BLK] for i in range(size))
            m_ref[...] = m_new
            acc_ref[...] = acc_ref[...] * fade + jnp.dot(
                p.astype(jnp.bfloat16), value_tile, preferred_element_type=jnp.float32
            )

        full = lax.div(jnp.maximum(count - 1, 0), CHUNK)

        def full_step(chunk, _):
            step(chunk * CHUNK, CHUNK, False)
            return 0

        lax.fori_loop(0, full, full_step, 0)
        rest = count - full * CHUNK
        for size in (4, 8, 12, 16):

            @pl.when((rest > size - 4) & (rest <= size))
            def _(size=size):
                step(full * CHUNK, size, True)

        lane = lax.broadcasted_iota(jnp.int32, (BLK, BLK), 1)
        stats = jnp.zeros((BLK, BLK), jnp.float32)
        for h in range(GROUP):
            part = slice(h * BLK, (h + 1) * BLK)
            total = jnp.sum(l_ref[part, :], axis=1, keepdims=True)
            safe = jnp.where(total > 0, total, 1.0)
            out_ref[q_rows, h * HD : (h + 1) * HD] = (acc_ref[part, :] / safe).astype(jnp.bfloat16)
            level = m_ref[part, :] + jnp.log2(safe)
            high = level.astype(jnp.bfloat16).astype(jnp.float32)
            middle = (level - high).astype(jnp.bfloat16).astype(jnp.float32)
            stats = jnp.where(lane == h, high, stats)
            stats = jnp.where(lane == 8 + h, middle, stats)
            stats = jnp.where(lane == 16 + h, level - high - middle, stats)
        out_ref[q_rows, FEATS:] = stats.astype(jnp.bfloat16)
        return 0

    def send_block(t, _):
        one_block(t, 0)
        for i in range(2):

            @pl.when(t == i)
            def _(i=i):
                out_copies[i].start()

        return 0

    lax.fori_loop(0, 2, send_block, 0)
    for copy in out_copies:
        copy.wait()


def attend(side, table, q, parts):
    part_rows = parts[0].shape[0]
    rows = GROUP * BLK
    return pl.pallas_call(
        functools.partial(attend_kernel, side),
        out_shape=jax.ShapeDtypeStruct((ROWS, FEATS + BLK), jnp.bfloat16),
        in_specs=[ANYWHERE] * 10,
        out_specs=ANYWHERE,
        scratch_shapes=[
            pltpu.SMEM((TABLE,), jnp.int32),
            pltpu.VMEM(q.shape, jnp.bfloat16),
            pltpu.VMEM((ROWS, FEATS + BLK), jnp.bfloat16),
            pltpu.VMEM((8 * part_rows, HD), jnp.bfloat16),
            pltpu.VMEM((rows, 2 * HD), jnp.bfloat16),
            pltpu.VMEM((rows, BLK), jnp.float32),
            pltpu.VMEM((rows, BLK), jnp.float32),
            pltpu.VMEM((rows, HD), jnp.float32),
            pltpu.SemaphoreType.DMA((8,)),
            pltpu.SemaphoreType.DMA((2,)),
            pltpu.SemaphoreType.DMA((2,)),
        ],
        compiler_params=pltpu.CompilerParams(vmem_limit_bytes=40 * 1024 * 1024),
        cost_estimate=pl.CostEstimate(flops=4_000_000_000, bytes_accessed=3_000_000, transcendentals=4_000_000),
        name="attend",
    )(table, q, *parts)


def project_kernel(table_ref, a_ref, b_ref, w_ref, keep_ref, send_ref, att_ref):
    my_zh, my_core = table_ref[HEAD_AT], table_ref[HEAD_AT + 1]

    @pl.when(pl.program_id(0) == 0)
    def _():
        stats_a = a_ref[:, FEATS:].astype(jnp.float32)
        stats_b = b_ref[:, FEATS:].astype(jnp.float32)
        for h in range(GROUP):

            def level(stats):
                return stats[:, h : h + 1] + stats[:, 8 + h : 9 + h] + stats[:, 16 + h : 17 + h]

            weight_a = 1.0 / (1.0 + jnp.exp2(level(stats_b) - level(stats_a)))
            cols = slice(h * HD, (h + 1) * HD)
            a, b = a_ref[:, cols].astype(jnp.float32), b_ref[:, cols].astype(jnp.float32)
            att_ref[:, cols] = (b + (a - b) * weight_a).astype(jnp.bfloat16)

    tile = keep_ref.shape[2]
    cols = pl.ds(pl.multiple_of(pl.program_id(0) * tile, tile), tile)
    res = jnp.dot(att_ref[...], w_ref[:, cols], preferred_element_type=jnp.float32).astype(jnp.bfloat16)
    for z in range(4):
        to = (z - my_zh) & 3
        zero, one = res[z * 64 : z * 64 + 32, :], res[z * 64 + 32 : z * 64 + 64, :]
        keep_ref[to] = jnp.where(my_core == 0, zero, one)
        send_ref[to] = jnp.where(my_core == 0, one, zero)


def project(table, a, b, w):
    out_cols = w.shape[1]
    tile = 512
    piece = jax.ShapeDtypeStruct((4, 32, out_cols), jnp.bfloat16)
    out_spec = pl.BlockSpec((4, 32, tile), lambda i: (0, 0, i))
    return pl.pallas_call(
        project_kernel,
        grid=(out_cols // tile,),
        out_shape=(piece, piece),
        in_specs=[
            SMEM,
            pl.BlockSpec(a.shape, lambda i: (0, 0)),
            pl.BlockSpec(b.shape, lambda i: (0, 0)),
            pl.BlockSpec(w.shape, lambda i: (0, 0)),
        ],
        out_specs=(out_spec, out_spec),
        scratch_shapes=[pltpu.VMEM((ROWS, FEATS), jnp.bfloat16)],
        compiler_params=pltpu.CompilerParams(vmem_limit_bytes=24 * 1024 * 1024),
        cost_estimate=pl.CostEstimate(flops=1_640_000_000, bytes_accessed=9_000_000, transcendentals=1792),
        name="project",
    )(table, a, b, w)


def body(queries, keys, values, out_weight, segment_info, block_order):
    k, v = keys[:, 0, :], values[:, 0, :]
    q = jnp.transpose(queries, (1, 0, 2))
    other_q = shift(q, "zl", 1)
    k = [k] + [shift(k, "y", o) for o in OFFSETS[1:]]
    v = [v] + [shift(v, "x", o) for o in OFFSETS[1:]]
    table = make_table(block_order, segment_info.T)
    k, v, table, other_q = lax.optimization_barrier((k, v, table, other_q))
    k = jnp.concatenate(k, axis=0)
    v = jnp.concatenate(v, axis=0)
    k, v = lax.optimization_barrier((k, v))
    parts = [k, v]
    for o in OFFSETS[1:]:
        parts += [shift(v, "y", o), shift(k, "x", o)]
    other = attend(0, table, other_q, parts)
    back = shift(other, "zl", 1)
    own = attend(1, table, q, parts)
    keep, send = project(table, own, back, out_weight)
    pieces = keep.astype(jnp.float32) + shift(send, "core", 1).astype(jnp.float32)
    low = pieces.astype(jnp.bfloat16)
    top, bottom = slice(0, 16), slice(16, 32)
    ahead = jnp.concatenate([low[2, top], low[1, bottom]], axis=0)
    back = jnp.concatenate([low[2, bottom], low[3, top]], axis=0)
    from_behind, from_ahead = shift(ahead, "zh", -1), shift(back, "zh", 1)
    ahead = (pieces[1, top] + from_behind[top].astype(jnp.float32)).astype(jnp.bfloat16)
    back = (pieces[3, bottom] + from_ahead[top].astype(jnp.float32)).astype(jnp.bfloat16)
    last_behind, last_ahead = shift(ahead, "zh", -1), shift(back, "zh", 1)
    behind = jnp.concatenate([last_behind, from_behind[bottom]], axis=0)
    beyond = jnp.concatenate([from_ahead[bottom], last_ahead], axis=0)
    total = pieces[0] + behind.astype(jnp.float32) + beyond.astype(jnp.float32)
    return total.astype(jnp.bfloat16)


def solution(mesh):
    fine = Mesh(mesh.devices.reshape(tuple(SIZES.values())), AXES)
    placed = (
        P(CTX, HEAD, None),
        P(CTX, HEAD, None),
        P(CTX, HEAD, None),
        P(HEAD, None),
        P(),
        P(),
    )
    return jax.shard_map(body, mesh=fine, in_specs=placed, out_specs=P(AXES, None), check_vma=False)
```

```python
import functools
import math

import jax
import jax.numpy as jnp
from jax import lax
from jax.experimental import pallas as pl
from jax.experimental.pallas import tpu as pltpu
from jax.sharding import Mesh, PartitionSpec as P

BLK = 128
HD = 128
GROUP = 7
ROWS = 256
FEATS = GROUP * HD
BLOCKS = 64
CHUNK = 16
LIST = 48
QUERY_AT = 3 * LIST
HEAD_AT = QUERY_AT + 16
TABLE = 256
W_TILES = 2
MINUS = -1e30
SIZES = {"x": 4, "zl": 2, "y": 4, "zh": 4, "core": 2}
AXES = tuple(SIZES)
CTX = ("x", "zl", "y")
HEAD = ("zh", "core")
OFFSETS = (0, 1, -1, 2)
PLACES = (0, 4, 5, 1, 6, 2, 7, 3)
SMEM = pl.BlockSpec(memory_space=pltpu.SMEM)
VMEM = pl.BlockSpec(memory_space=pltpu.VMEM)
ANYWHERE = pl.BlockSpec(memory_space=pl.ANY)


def shift(value, axis, step):
    size = SIZES[axis]
    return lax.ppermute(value, axis, [((i + step) % size, i) for i in range(size)])


def table_kernel(order_ref, info_ref, out_ref, table_ref, inv_ref, sem):
    my_x, my_zl, my_y = (lax.axis_index(axis) for axis in CTX)

    def invert(block, _):
        inv_ref[order_ref[block]] = block
        return 0

    lax.fori_loop(0, BLOCKS, invert, 0)
    table_ref[HEAD_AT] = lax.axis_index("zh")
    table_ref[HEAD_AT + 1] = lax.axis_index("core")
    ends = []
    for i in range(4):
        pair_zl = my_zl ^ 1 if i < 2 else my_zl
        block = order_ref[((my_x * 2 + pair_zl) * 4 + my_y) * 2 + i % 2]
        last, kind = info_ref[1, block], info_ref[2, block]
        at = QUERY_AT + 4 * i
        table_ref[at], table_ref[at + 1], table_ref[at + 2] = block, kind, last
        ends.append(jnp.where(kind == 1, lax.div(last, BLK) - 1, block))

    def place(position, carry):
        count, seen = carry[0], carry[1:]
        block = inv_ref[position]
        ctx = block >> 1
        x_off, y_off = ((ctx >> 3) - my_x) & 3, ((ctx & 3) - my_y) & 3
        x_part, y_part = (x_off ^ (x_off >> 1)), (y_off ^ (y_off >> 1))
        here = ((ctx >> 2) & 1) == my_zl
        table_ref[count] = (x_part * 4 + y_part) * 2 + (block & 1)
        table_ref[LIST + count] = (y_part * 4 + x_part) * 2 + (block & 1)
        table_ref[2 * LIST + count] = position
        count = count + here.astype(jnp.int32)
        return (count,) + tuple(jnp.where(position == end, count, s) for end, s in zip(ends, seen))

    done = lax.fori_loop(0, BLOCKS, place, (jnp.int32(0),) * 5)
    for i in range(4):
        table_ref[QUERY_AT + 4 * i + 3] = done[1 + i]
    for i in range(BLOCKS // 2, LIST):
        table_ref[i] = 0
        table_ref[LIST + i] = 0
        table_ref[2 * LIST + i] = BLOCKS
    copy = pltpu.make_async_copy(table_ref, out_ref, sem)
    copy.start()
    copy.wait()


def make_table(order, info):
    return pl.pallas_call(
        table_kernel,
        out_shape=jax.ShapeDtypeStruct((TABLE,), jnp.int32),
        in_specs=[SMEM, SMEM],
        out_specs=ANYWHERE,
        scratch_shapes=[
            pltpu.SMEM((TABLE,), jnp.int32),
            pltpu.SMEM((BLOCKS,), jnp.int32),
            pltpu.SemaphoreType.DMA,
        ],
        cost_estimate=pl.CostEstimate(flops=2_000_000_000, bytes_accessed=1000, transcendentals=0),
        name="table",
    )(order, info)


def attend_kernel(side, table_hbm, q_hbm, *refs):
    parts, refs = refs[:8], refs[8:]
    out_hbm, *refs = refs
    table_ref, q_ref, out_ref, kv_ref, qs_ref, m_ref, l_ref, acc_ref, kv_sem, in_sem, out_sem = refs
    part_rows = parts[0].shape[0]
    half = 4 * part_rows
    table_copy = pltpu.make_async_copy(table_hbm, table_ref, in_sem.at[0])
    q_copy = pltpu.make_async_copy(q_hbm, q_ref, in_sem.at[1])
    copies = [
        pltpu.make_async_copy(part, kv_ref.at[pl.ds(i * part_rows, part_rows)], kv_sem.at[i])
        for i, part in zip(PLACES, parts)
    ]
    out_copies = [
        pltpu.make_async_copy(
            out_ref.at[pl.ds(t * BLK, BLK)], out_hbm.at[pl.ds(t * BLK, BLK)], out_sem.at[t]
        )
        for t in range(2)
    ]
    table_copy.start()
    q_copy.start()
    for copy in copies:
        copy.start()
    scale = math.log2(math.e) / math.sqrt(HD)
    rows = GROUP * BLK
    q_copy.wait()
    table_copy.wait()
    for copy in copies:
        copy.wait()

    def one_block(t, _):
        at = QUERY_AT + 4 * (2 * side + t)
        block, kind, last, count = table_ref[at], table_ref[at + 1], table_ref[at + 2], table_ref[at + 3]
        q_rows = pl.ds(pl.multiple_of(t * BLK, BLK), BLK)
        for h in range(GROUP):
            scaled = q_ref[h, q_rows, :].astype(jnp.float32) * scale
            high = scaled.astype(jnp.bfloat16)
            qs_ref[h * BLK : (h + 1) * BLK, 0:HD] = high
            qs_ref[h * BLK : (h + 1) * BLK, HD:] = (scaled - high.astype(jnp.float32)).astype(jnp.bfloat16)
        m_ref[...] = jnp.full_like(m_ref, MINUS)
        l_ref[...] = jnp.zeros_like(l_ref)
        acc_ref[...] = jnp.zeros_like(acc_ref)

        def step(begin, size, masked):
            key_list, value_list = [], []
            for j in range(size):
                key_at = pl.multiple_of(table_ref[begin + j] * BLK, BLK)
                value_at = pl.multiple_of(table_ref[LIST + begin + j] * BLK, BLK)
                key_list.append(kv_ref[pl.ds(key_at, BLK), :])
                value_list.append(kv_ref[pl.ds(value_at + half, BLK), :])
            key_tile = jnp.concatenate(key_list, axis=0)
            value_tile = jnp.concatenate(value_list, axis=0)
            twice = jnp.concatenate([key_tile, key_tile], axis=1)
            s = lax.dot_general(
                qs_ref[...], twice, (((1,), (1,)), ((), ())), preferred_element_type=jnp.float32
            )
            if masked:
                lane = lax.broadcasted_iota(jnp.int32, (rows, BLK), 1)
                row = lax.broadcasted_iota(jnp.int32, (rows, BLK), 0) & (BLK - 1)
                most = jnp.where(kind == 1, last - 1, block * BLK + row) - lane
                s = jnp.concatenate(
                    [
                        jnp.where(
                            table_ref[2 * LIST + begin + j] * BLK <= most, s[:, j * BLK : (j + 1) * BLK], MINUS
                        )
                        for j in range(size)
                    ],
                    axis=1,
                )
            m_old = m_ref[...]
            m_new = jnp.maximum(m_old, jnp.max(s, axis=1, keepdims=True))
            p = jnp.exp2(s - jnp.concatenate([m_new] * size, axis=1))
            fade = jnp.exp2(m_old - m_new)
            l_ref[...] = l_ref[...] * fade + sum(p[:, i * BLK : (i + 1) * BLK] for i in range(size))
            m_ref[...] = m_new
            acc_ref[...] = acc_ref[...] * fade + jnp.dot(
                p.astype(jnp.bfloat16), value_tile, preferred_element_type=jnp.float32
            )

        full = lax.div(jnp.maximum(count - 1, 0), CHUNK)

        def full_step(chunk, _):
            step(chunk * CHUNK, CHUNK, False)
            return 0

        lax.fori_loop(0, full, full_step, 0)
        rest = count - full * CHUNK
        for size in (4, 8, 12, 16):

            @pl.when((rest > size - 4) & (rest <= size))
            def _(size=size):
                step(full * CHUNK, size, True)

        lane = lax.broadcasted_iota(jnp.int32, (BLK, BLK), 1)
        stats = jnp.zeros((BLK, BLK), jnp.float32)
        for h in range(GROUP):
            part = slice(h * BLK, (h + 1) * BLK)
            total = jnp.sum(l_ref[part, :], axis=1, keepdims=True)
            safe = jnp.where(total > 0, total, 1.0)
            out_ref[q_rows, h * HD : (h + 1) * HD] = (acc_ref[part, :] / safe).astype(jnp.bfloat16)
            level = m_ref[part, :] + jnp.log2(safe)
            high = level.astype(jnp.bfloat16).astype(jnp.float32)
            middle = (level - high).astype(jnp.bfloat16).astype(jnp.float32)
            stats = jnp.where(lane == h, high, stats)
            stats = jnp.where(lane == 8 + h, middle, stats)
            stats = jnp.where(lane == 16 + h, level - high - middle, stats)
        out_ref[q_rows, FEATS:] = stats.astype(jnp.bfloat16)
        return 0

    def send_block(t, _):
        one_block(t, 0)
        for i in range(2):

            @pl.when(t == i)
            def _(i=i):
                out_copies[i].start()

        return 0

    lax.fori_loop(0, 2, send_block, 0)
    for copy in out_copies:
        copy.wait()


def attend(side, table, q, parts):
    part_rows = parts[0].shape[0]
    rows = GROUP * BLK
    return pl.pallas_call(
        functools.partial(attend_kernel, side),
        out_shape=(jax.ShapeDtypeStruct((ROWS, FEATS + BLK), jnp.bfloat16),),
        in_specs=[ANYWHERE] * 10,
        out_specs=(ANYWHERE,),
        scratch_shapes=[
            pltpu.SMEM((TABLE,), jnp.int32),
            pltpu.VMEM(q.shape, jnp.bfloat16),
            pltpu.VMEM((ROWS, FEATS + BLK), jnp.bfloat16),
            pltpu.VMEM((8 * part_rows, HD), jnp.bfloat16),
            pltpu.VMEM((rows, 2 * HD), jnp.bfloat16),
            pltpu.VMEM((rows, BLK), jnp.float32),
            pltpu.VMEM((rows, BLK), jnp.float32),
            pltpu.VMEM((rows, HD), jnp.float32),
            pltpu.SemaphoreType.DMA((8,)),
            pltpu.SemaphoreType.DMA((2,)),
            pltpu.SemaphoreType.DMA((2,)),
        ],
        compiler_params=pltpu.CompilerParams(vmem_limit_bytes=32 * 1024 * 1024),
        cost_estimate=pl.CostEstimate(flops=4_000_000_000, bytes_accessed=3_000_000, transcendentals=4_000_000),
        name="attend",
    )(table, q, *parts)


def project_kernel(table_hbm, a_hbm, b_hbm, w_ref, keep_ref, send_ref, table_ref, a_ref, b_ref, att_ref, in_sem):
    tile = w_ref.shape[1] // W_TILES
    in_copies = [
        pltpu.make_async_copy(source, target, in_sem.at[i])
        for i, (source, target) in enumerate(((table_hbm, table_ref), (a_hbm, a_ref), (b_hbm, b_ref)))
    ]
    for copy in in_copies:
        copy.start()
    for copy in in_copies:
        copy.wait()
    my_zh, my_core = table_ref[HEAD_AT], table_ref[HEAD_AT + 1]
    stats_a = a_ref[:, FEATS:].astype(jnp.float32)
    stats_b = b_ref[:, FEATS:].astype(jnp.float32)
    gap = stats_b - stats_a
    for h in range(GROUP):
        levels = gap[:, h : h + 1] + gap[:, 8 + h : 9 + h] + gap[:, 16 + h : 17 + h]
        weight_a = 1.0 / (1.0 + jnp.exp2(jnp.broadcast_to(levels, (ROWS, HD))))
        cols = slice(h * HD, (h + 1) * HD)
        a, b = a_ref[:, cols].astype(jnp.float32), b_ref[:, cols].astype(jnp.float32)
        att_ref[:, cols] = (b + (a - b) * weight_a).astype(jnp.bfloat16)
    for i in range(W_TILES):
        cols = slice(i * tile, (i + 1) * tile)
        res = jnp.dot(att_ref[...], w_ref[:, cols], preferred_element_type=jnp.float32).astype(jnp.bfloat16)
        for z in range(4):
            to = (z - my_zh) & 3
            zero, one = res[z * 64 : z * 64 + 32, :], res[z * 64 + 32 : z * 64 + 64, :]
            keep_ref[to, :, cols] = jnp.where(my_core == 0, zero, one)
            send_ref[to, :, cols] = jnp.where(my_core == 0, one, zero)


def project(table, a, b, w):
    piece = jax.ShapeDtypeStruct((4, 32, w.shape[1]), jnp.bfloat16)
    return pl.pallas_call(
        project_kernel,
        out_shape=(piece, piece),
        in_specs=[ANYWHERE] * 3 + [VMEM],
        out_specs=(VMEM, VMEM),
        scratch_shapes=[
            pltpu.SMEM((TABLE,), jnp.int32),
            pltpu.VMEM(a.shape, jnp.bfloat16),
            pltpu.VMEM(b.shape, jnp.bfloat16),
            pltpu.VMEM((ROWS, FEATS), jnp.bfloat16),
            pltpu.SemaphoreType.DMA((3,)),
        ],
        compiler_params=pltpu.CompilerParams(vmem_limit_bytes=20 * 1024 * 1024),
        cost_estimate=pl.CostEstimate(flops=1_640_000_000, bytes_accessed=9_000_000, transcendentals=1792),
        name="project",
    )(table, a, b, w)


def body(queries, keys, values, out_weight, segment_info, block_order):
    k, v = keys[:, 0, :], values[:, 0, :]
    q = jnp.transpose(queries, (1, 0, 2))
    other_q = shift(q, "zl", 1)
    k = [k] + [shift(k, "y", o) for o in OFFSETS[1:]]
    v = [v] + [shift(v, "x", o) for o in OFFSETS[1:]]
    table = make_table(block_order, segment_info.T)
    k, v, table, other_q = lax.optimization_barrier((k, v, table, other_q))
    k = jnp.concatenate(k, axis=0)
    v = jnp.concatenate(v, axis=0)
    k, v = lax.optimization_barrier((k, v))
    parts = [k, v]
    for o in OFFSETS[1:]:
        parts += lax.optimization_barrier((shift(v, "y", o), shift(k, "x", o)))
    (other,) = attend(0, table, other_q, parts)
    back = shift(other, "zl", 1)
    (own,) = attend(1, table, q, parts)
    keep, send = project(table, own, back, out_weight)
    pieces = keep.astype(jnp.float32) + shift(send, "core", 1).astype(jnp.float32)
    low = pieces.astype(jnp.bfloat16)
    top, bottom = slice(0, 16), slice(16, 32)
    ahead = jnp.concatenate([low[2, top], low[1, bottom]], axis=0)
    back = jnp.concatenate([low[2, bottom], low[3, top]], axis=0)
    from_behind, from_ahead = shift(ahead, "zh", -1), shift(back, "zh", 1)
    ahead = (pieces[1, top] + from_behind[top].astype(jnp.float32)).astype(jnp.bfloat16)
    back = (pieces[3, bottom] + from_ahead[top].astype(jnp.float32)).astype(jnp.bfloat16)
    last_behind, last_ahead = shift(ahead, "zh", -1), shift(back, "zh", 1)
    behind = jnp.concatenate([last_behind, from_behind[bottom]], axis=0)
    beyond = jnp.concatenate([from_ahead[bottom], last_ahead], axis=0)
    total = pieces[0] + behind.astype(jnp.float32) + beyond.astype(jnp.float32)
    return total.astype(jnp.bfloat16)


def solution(mesh):
    fine = Mesh(mesh.devices.reshape(tuple(SIZES.values())), AXES)
    placed = (
        P(CTX, HEAD, None),
        P(CTX, HEAD, None),
        P(CTX, HEAD, None),
        P(HEAD, None),
        P(),
        P(),
    )
    return jax.shard_map(body, mesh=fine, in_specs=placed, out_specs=P(AXES, None), check_vma=False)
```

```python
import functools
import math

import jax
import jax.numpy as jnp
from jax import lax
from jax.experimental import pallas as pl
from jax.experimental.pallas import tpu as pltpu
from jax.sharding import Mesh, PartitionSpec as P

BLK = 128
HD = 128
GROUP = 7
ROWS = 256
FEATS = GROUP * HD
BLOCKS = 64
CHUNK = 16
LIST = 48
QUERY_AT = 3 * LIST
HEAD_AT = QUERY_AT + 16
TABLE = 256
W_TILES = 2
MINUS = -1e30
SIZES = {"x": 4, "zl": 2, "y": 4, "zh": 4, "core": 2}
AXES = tuple(SIZES)
CTX = ("x", "zl", "y")
HEAD = ("zh", "core")
OFFSETS = (0, 1, -1, 2)
PLACES = (0, 4, 5, 1, 6, 2, 7, 3)
SMEM = pl.BlockSpec(memory_space=pltpu.SMEM)
VMEM = pl.BlockSpec(memory_space=pltpu.VMEM)
ANYWHERE = pl.BlockSpec(memory_space=pl.ANY)


def shift(value, axis, step):
    size = SIZES[axis]
    return lax.ppermute(value, axis, [((i + step) % size, i) for i in range(size)])


def table_kernel(order_ref, info_ref, out_ref, table_ref, inv_ref, sem):
    my_x, my_zl, my_y = (lax.axis_index(axis) for axis in CTX)

    def invert(block, _):
        inv_ref[order_ref[block]] = block
        return 0

    lax.fori_loop(0, BLOCKS, invert, 0)
    table_ref[HEAD_AT] = lax.axis_index("zh")
    table_ref[HEAD_AT + 1] = lax.axis_index("core")
    ends = []
    for i in range(4):
        pair_zl = my_zl ^ 1 if i < 2 else my_zl
        block = order_ref[((my_x * 2 + pair_zl) * 4 + my_y) * 2 + i % 2]
        last, kind = info_ref[1, block], info_ref[2, block]
        at = QUERY_AT + 4 * i
        table_ref[at], table_ref[at + 1], table_ref[at + 2] = block, kind, last
        ends.append(jnp.where(kind == 1, lax.div(last, BLK) - 1, block))

    def place(position, carry):
        count, seen = carry[0], carry[1:]
        block = inv_ref[position]
        ctx = block >> 1
        x_off, y_off = ((ctx >> 3) - my_x) & 3, ((ctx & 3) - my_y) & 3
        x_part, y_part = (x_off ^ (x_off >> 1)), (y_off ^ (y_off >> 1))
        here = ((ctx >> 2) & 1) == my_zl
        table_ref[count] = (x_part * 4 + y_part) * 2 + (block & 1)
        table_ref[LIST + count] = (y_part * 4 + x_part) * 2 + (block & 1)
        table_ref[2 * LIST + count] = position
        count = count + here.astype(jnp.int32)
        return (count,) + tuple(jnp.where(position == end, count, s) for end, s in zip(ends, seen))

    done = lax.fori_loop(0, BLOCKS, place, (jnp.int32(0),) * 5)
    for i in range(4):
        table_ref[QUERY_AT + 4 * i + 3] = done[1 + i]
    for i in range(BLOCKS // 2, LIST):
        table_ref[i] = 0
        table_ref[LIST + i] = 0
        table_ref[2 * LIST + i] = BLOCKS
    copy = pltpu.make_async_copy(table_ref, out_ref, sem)
    copy.start()
    copy.wait()


def make_table(order, info):
    return pl.pallas_call(
        table_kernel,
        out_shape=jax.ShapeDtypeStruct((TABLE,), jnp.int32),
        in_specs=[SMEM, SMEM],
        out_specs=ANYWHERE,
        scratch_shapes=[
            pltpu.SMEM((TABLE,), jnp.int32),
            pltpu.SMEM((BLOCKS,), jnp.int32),
            pltpu.SemaphoreType.DMA,
        ],
        cost_estimate=pl.CostEstimate(flops=2_000_000_000, bytes_accessed=1000, transcendentals=0),
        name="table",
    )(order, info)


def attend_kernel(side, table_hbm, q_hbm, *refs):
    parts, refs = refs[:8], refs[8:]
    out_hbm, *refs = refs
    table_ref, q_ref, out_ref, kv_ref, qs_ref, m_ref, l_ref, acc_ref, kv_sem, in_sem, out_sem = refs
    part_rows = parts[0].shape[0]
    half = 4 * part_rows
    table_copy = pltpu.make_async_copy(table_hbm, table_ref, in_sem.at[0])
    q_copy = pltpu.make_async_copy(q_hbm, q_ref, in_sem.at[1])
    copies = [
        pltpu.make_async_copy(part, kv_ref.at[pl.ds(i * part_rows, part_rows)], kv_sem.at[i])
        for i, part in zip(PLACES, parts)
    ]
    out_copies = [
        pltpu.make_async_copy(
            out_ref.at[pl.ds(t * BLK, BLK)], out_hbm.at[pl.ds(t * BLK, BLK)], out_sem.at[t]
        )
        for t in range(2)
    ]
    table_copy.start()
    q_copy.start()
    for copy in copies:
        copy.start()
    scale = math.log2(math.e) / math.sqrt(HD)
    rows = GROUP * BLK
    q_copy.wait()
    table_copy.wait()
    for copy in copies:
        copy.wait()

    def one_block(t, _):
        at = QUERY_AT + 4 * (2 * side + t)
        block, kind, last, count = table_ref[at], table_ref[at + 1], table_ref[at + 2], table_ref[at + 3]
        q_rows = pl.ds(pl.multiple_of(t * BLK, BLK), BLK)
        for h in range(GROUP):
            scaled = q_ref[h, q_rows, :].astype(jnp.float32) * scale
            high = scaled.astype(jnp.bfloat16)
            qs_ref[h * BLK : (h + 1) * BLK, 0:HD] = high
            qs_ref[h * BLK : (h + 1) * BLK, HD:] = (scaled - high.astype(jnp.float32)).astype(jnp.bfloat16)
        m_ref[...] = jnp.full_like(m_ref, MINUS)
        l_ref[...] = jnp.zeros_like(l_ref)
        acc_ref[...] = jnp.zeros_like(acc_ref)

        def step(begin, size, masked):
            key_list, value_list = [], []
            for j in range(size):
                key_at = pl.multiple_of(table_ref[begin + j] * BLK, BLK)
                value_at = pl.multiple_of(table_ref[LIST + begin + j] * BLK, BLK)
                key_list.append(kv_ref[pl.ds(key_at, BLK), :])
                value_list.append(kv_ref[pl.ds(value_at + half, BLK), :])
            key_tile = jnp.concatenate(key_list, axis=0)
            value_tile = jnp.concatenate(value_list, axis=0)
            twice = jnp.concatenate([key_tile, key_tile], axis=1)
            s = lax.dot_general(
                qs_ref[...], twice, (((1,), (1,)), ((), ())), preferred_element_type=jnp.float32
            )
            if masked:
                lane = lax.broadcasted_iota(jnp.int32, (rows, BLK), 1)
                row = lax.broadcasted_iota(jnp.int32, (rows, BLK), 0) & (BLK - 1)
                most = jnp.where(kind == 1, last - 1, block * BLK + row) - lane
                s = jnp.concatenate(
                    [
                        jnp.where(
                            table_ref[2 * LIST + begin + j] * BLK <= most, s[:, j * BLK : (j + 1) * BLK], MINUS
                        )
                        for j in range(size)
                    ],
                    axis=1,
                )
            m_old = m_ref[...]
            m_new = jnp.maximum(m_old, jnp.max(s, axis=1, keepdims=True))
            p = jnp.exp2(s - jnp.concatenate([m_new] * size, axis=1))
            fade = jnp.exp2(m_old - m_new)
            l_ref[...] = l_ref[...] * fade + sum(p[:, i * BLK : (i + 1) * BLK] for i in range(size))
            m_ref[...] = m_new
            acc_ref[...] = acc_ref[...] * fade + jnp.dot(
                p.astype(jnp.bfloat16), value_tile, preferred_element_type=jnp.float32
            )

        full = lax.div(jnp.maximum(count - 1, 0), CHUNK)

        def full_step(chunk, _):
            step(chunk * CHUNK, CHUNK, False)
            return 0

        lax.fori_loop(0, full, full_step, 0)
        rest = count - full * CHUNK
        for size in (4, 8, 12, 16):

            @pl.when((rest > size - 4) & (rest <= size))
            def _(size=size):
                step(full * CHUNK, size, True)

        lane = lax.broadcasted_iota(jnp.int32, (BLK, BLK), 1)
        stats = jnp.zeros((BLK, BLK), jnp.float32)
        for h in range(GROUP):
            part = slice(h * BLK, (h + 1) * BLK)
            total = jnp.sum(l_ref[part, :], axis=1, keepdims=True)
            safe = jnp.where(total > 0, total, 1.0)
            out_ref[q_rows, h * HD : (h + 1) * HD] = (acc_ref[part, :] / safe).astype(jnp.bfloat16)
            level = m_ref[part, :] + jnp.log2(safe)
            high = level.astype(jnp.bfloat16).astype(jnp.float32)
            middle = (level - high).astype(jnp.bfloat16).astype(jnp.float32)
            stats = jnp.where(lane == h, high, stats)
            stats = jnp.where(lane == 8 + h, middle, stats)
            stats = jnp.where(lane == 16 + h, level - high - middle, stats)
        out_ref[q_rows, FEATS:] = stats.astype(jnp.bfloat16)
        return 0

    def send_block(t, _):
        one_block(t, 0)
        for i in range(2):

            @pl.when(t == i)
            def _(i=i):
                out_copies[i].start()

        return 0

    lax.fori_loop(0, 2, send_block, 0)
    for copy in out_copies:
        copy.wait()


def attend(side, table, q, parts):
    part_rows = parts[0].shape[0]
    rows = GROUP * BLK
    return pl.pallas_call(
        functools.partial(attend_kernel, side),
        out_shape=(jax.ShapeDtypeStruct((ROWS, FEATS + BLK), jnp.bfloat16),),
        in_specs=[ANYWHERE] * 10,
        out_specs=(ANYWHERE,),
        scratch_shapes=[
            pltpu.SMEM((TABLE,), jnp.int32),
            pltpu.VMEM(q.shape, jnp.bfloat16),
            pltpu.VMEM((ROWS, FEATS + BLK), jnp.bfloat16),
            pltpu.VMEM((8 * part_rows, HD), jnp.bfloat16),
            pltpu.VMEM((rows, 2 * HD), jnp.bfloat16),
            pltpu.VMEM((rows, BLK), jnp.float32),
            pltpu.VMEM((rows, BLK), jnp.float32),
            pltpu.VMEM((rows, HD), jnp.float32),
            pltpu.SemaphoreType.DMA((8,)),
            pltpu.SemaphoreType.DMA((2,)),
            pltpu.SemaphoreType.DMA((2,)),
        ],
        compiler_params=pltpu.CompilerParams(vmem_limit_bytes=32 * 1024 * 1024),
        cost_estimate=pl.CostEstimate(flops=4_000_000_000, bytes_accessed=3_000_000, transcendentals=4_000_000),
        name="attend",
    )(table, q, *parts)


def project_kernel(table_hbm, a_hbm, b_hbm, w_ref, keep_ref, send_ref, table_ref, a_ref, b_ref, att_ref, in_sem):
    tile = w_ref.shape[1] // W_TILES
    in_copies = [
        pltpu.make_async_copy(source, target, in_sem.at[i])
        for i, (source, target) in enumerate(((table_hbm, table_ref), (a_hbm, a_ref), (b_hbm, b_ref)))
    ]
    for copy in in_copies:
        copy.start()
    for copy in in_copies:
        copy.wait()
    my_zh, my_core = table_ref[HEAD_AT], table_ref[HEAD_AT + 1]
    stats_a = a_ref[:, FEATS:].astype(jnp.float32)
    stats_b = b_ref[:, FEATS:].astype(jnp.float32)
    gap = stats_b - stats_a
    for h in range(GROUP):
        levels = gap[:, h : h + 1] + gap[:, 8 + h : 9 + h] + gap[:, 16 + h : 17 + h]
        weight_a = 1.0 / (1.0 + jnp.exp2(jnp.broadcast_to(levels, (ROWS, HD))))
        cols = slice(h * HD, (h + 1) * HD)
        a, b = a_ref[:, cols].astype(jnp.float32), b_ref[:, cols].astype(jnp.float32)
        att_ref[:, cols] = (b + (a - b) * weight_a).astype(jnp.bfloat16)
    for i in range(W_TILES):
        cols = slice(i * tile, (i + 1) * tile)
        res = jnp.dot(att_ref[...], w_ref[:, cols], preferred_element_type=jnp.float32).astype(jnp.bfloat16)
        for z in range(4):
            to = (z - my_zh) & 3
            zero, one = res[z * 64 : z * 64 + 32, :], res[z * 64 + 32 : z * 64 + 64, :]
            keep_ref[to, :, cols] = jnp.where(my_core == 0, zero, one)
            send_ref[to, :, cols] = jnp.where(my_core == 0, one, zero)


def project(table, a, b, w):
    piece = jax.ShapeDtypeStruct((4, 32, w.shape[1]), jnp.bfloat16)
    return pl.pallas_call(
        project_kernel,
        out_shape=(piece, piece),
        in_specs=[ANYWHERE] * 3 + [VMEM],
        out_specs=(VMEM, VMEM),
        scratch_shapes=[
            pltpu.SMEM((TABLE,), jnp.int32),
            pltpu.VMEM(a.shape, jnp.bfloat16),
            pltpu.VMEM(b.shape, jnp.bfloat16),
            pltpu.VMEM((ROWS, FEATS), jnp.bfloat16),
            pltpu.SemaphoreType.DMA((3,)),
        ],
        compiler_params=pltpu.CompilerParams(vmem_limit_bytes=20 * 1024 * 1024),
        cost_estimate=pl.CostEstimate(flops=1_640_000_000, bytes_accessed=9_000_000, transcendentals=1792),
        name="project",
    )(table, a, b, w)


def body(queries, keys, values, out_weight, segment_info, block_order):
    k, v = keys[:, 0, :], values[:, 0, :]
    q = jnp.transpose(queries, (1, 0, 2))
    other_q = shift(q, "zl", 1)
    k = [k] + [shift(k, "y", o) for o in OFFSETS[1:]]
    v = [v] + [shift(v, "x", o) for o in OFFSETS[1:]]
    table = jnp.minimum(make_table(block_order, segment_info.T), 1 << 20)
    k, other_q = lax.optimization_barrier((k, other_q))
    k = jnp.concatenate(k, axis=0)
    v = jnp.concatenate(v, axis=0)
    parts = [k, v]
    for o in OFFSETS[1:]:
        parts += lax.optimization_barrier((shift(v, "y", o), shift(k, "x", o)))
    (other,) = attend(0, table, other_q, parts)
    back = shift(other, "zl", 1)
    (own,) = attend(1, table, q, parts)
    keep, send = project(table, own, back, out_weight)
    pieces = keep.astype(jnp.float32) + shift(send, "core", 1).astype(jnp.float32)
    low = pieces.astype(jnp.bfloat16)
    top, bottom = slice(0, 16), slice(16, 32)
    from_behind, from_ahead = lax.optimization_barrier((shift(low[2, top], "zh", -1), shift(low[2, bottom], "zh", 1)))
    ahead = (pieces[1, top] + from_behind.astype(jnp.float32)).astype(jnp.bfloat16)
    back = (pieces[3, bottom] + from_ahead.astype(jnp.float32)).astype(jnp.bfloat16)
    behind = [shift(ahead, "zh", -1), shift(low[1, bottom], "zh", -1)]
    beyond = [shift(low[3, top], "zh", 1), shift(back, "zh", 1)]
    behind, beyond = jnp.concatenate(behind, axis=0), jnp.concatenate(beyond, axis=0)
    total = pieces[0] + behind.astype(jnp.float32) + beyond.astype(jnp.float32)
    return total.astype(jnp.bfloat16)


def solution(mesh):
    fine = Mesh(mesh.devices.reshape(tuple(SIZES.values())), AXES)
    placed = (
        P(CTX, HEAD, None),
        P(CTX, HEAD, None),
        P(CTX, HEAD, None),
        P(HEAD, None),
        P(),
        P(),
    )
    return jax.shard_map(body, mesh=fine, in_specs=placed, out_specs=P(AXES, None), check_vma=False)
```

```python
import functools
import math

import jax
import jax.numpy as jnp
from jax import lax
from jax.experimental import pallas as pl
from jax.experimental.pallas import tpu as pltpu
from jax.sharding import Mesh, PartitionSpec as P

BLK = 128
HD = 128
GROUP = 7
ROWS = 256
FEATS = GROUP * HD
BLOCKS = 64
CHUNK = 16
LIST = 48
QUERY_AT = 3 * LIST
HEAD_AT = QUERY_AT + 16
TABLE = 256
W_TILES = 2
MINUS = -1e30
SIZES = {"x": 4, "zl": 2, "y": 4, "zh": 4, "core": 2}
AXES = tuple(SIZES)
CTX = ("x", "zl", "y")
HEAD = ("zh", "core")
OFFSETS = (0, 1, -1, 2)
PLACES = (0, 4, 5, 1, 6, 2, 7, 3)
SMEM = pl.BlockSpec(memory_space=pltpu.SMEM)
VMEM = pl.BlockSpec(memory_space=pltpu.VMEM)
ANYWHERE = pl.BlockSpec(memory_space=pl.ANY)


def shift(value, axis, step):
    size = SIZES[axis]
    return lax.ppermute(value, axis, [((i + step) % size, i) for i in range(size)])


def table_kernel(order_ref, info_ref, out_ref, table_ref, inv_ref, sem):
    my_x, my_zl, my_y = (lax.axis_index(axis) for axis in CTX)

    def invert(block, _):
        inv_ref[order_ref[block]] = block
        return 0

    lax.fori_loop(0, BLOCKS, invert, 0)
    table_ref[HEAD_AT] = lax.axis_index("zh")
    table_ref[HEAD_AT + 1] = lax.axis_index("core")
    ends = []
    for i in range(4):
        pair_zl = my_zl ^ 1 if i < 2 else my_zl
        block = order_ref[((my_x * 2 + pair_zl) * 4 + my_y) * 2 + i % 2]
        last, kind = info_ref[1, block], info_ref[2, block]
        at = QUERY_AT + 4 * i
        table_ref[at], table_ref[at + 1], table_ref[at + 2] = block, kind, last
        ends.append(jnp.where(kind == 1, lax.div(last, BLK) - 1, block))

    def place(position, carry):
        count, seen = carry[0], carry[1:]
        block = inv_ref[position]
        ctx = block >> 1
        x_off, y_off = ((ctx >> 3) - my_x) & 3, ((ctx & 3) - my_y) & 3
        x_part, y_part = (x_off ^ (x_off >> 1)), (y_off ^ (y_off >> 1))
        here = ((ctx >> 2) & 1) == my_zl
        table_ref[count] = (x_part * 4 + y_part) * 2 + (block & 1)
        table_ref[LIST + count] = (y_part * 4 + x_part) * 2 + (block & 1)
        table_ref[2 * LIST + count] = position
        count = count + here.astype(jnp.int32)
        return (count,) + tuple(jnp.where(position == end, count, s) for end, s in zip(ends, seen))

    done = lax.fori_loop(0, BLOCKS, place, (jnp.int32(0),) * 5)
    for i in range(4):
        table_ref[QUERY_AT + 4 * i + 3] = done[1 + i]
    for i in range(BLOCKS // 2, LIST):
        table_ref[i] = 0
        table_ref[LIST + i] = 0
        table_ref[2 * LIST + i] = BLOCKS
    copy = pltpu.make_async_copy(table_ref, out_ref, sem)
    copy.start()
    copy.wait()


def make_table(order, info):
    return pl.pallas_call(
        table_kernel,
        out_shape=jax.ShapeDtypeStruct((TABLE,), jnp.int32),
        in_specs=[SMEM, SMEM],
        out_specs=ANYWHERE,
        scratch_shapes=[
            pltpu.SMEM((TABLE,), jnp.int32),
            pltpu.SMEM((BLOCKS,), jnp.int32),
            pltpu.SemaphoreType.DMA,
        ],
        cost_estimate=pl.CostEstimate(flops=2_000_000_000, bytes_accessed=1000, transcendentals=0),
        name="table",
    )(order, info)


def attend_kernel(side, table_hbm, q_hbm, *refs):
    parts, refs = refs[:8], refs[8:]
    out_hbm, *refs = refs
    table_ref, q_ref, out_ref, kv_ref, qs_ref, m_ref, l_ref, acc_ref, kv_sem, in_sem, out_sem = refs
    part_rows = parts[0].shape[0]
    half = 4 * part_rows
    table_copy = pltpu.make_async_copy(table_hbm, table_ref, in_sem.at[0])
    q_copy = pltpu.make_async_copy(q_hbm, q_ref, in_sem.at[1])
    copies = [
        pltpu.make_async_copy(part, kv_ref.at[pl.ds(i * part_rows, part_rows)], kv_sem.at[i])
        for i, part in zip(PLACES, parts)
    ]
    out_copies = [
        pltpu.make_async_copy(
            out_ref.at[pl.ds(t * BLK, BLK)], out_hbm.at[pl.ds(t * BLK, BLK)], out_sem.at[t]
        )
        for t in range(2)
    ]
    table_copy.start()
    q_copy.start()
    for copy in copies:
        copy.start()
    scale = math.log2(math.e) / math.sqrt(HD)
    rows = GROUP * BLK
    q_copy.wait()
    table_copy.wait()
    for copy in copies:
        copy.wait()

    def one_block(t, _):
        at = QUERY_AT + 4 * (2 * side + t)
        block, kind, last, count = table_ref[at], table_ref[at + 1], table_ref[at + 2], table_ref[at + 3]
        q_rows = pl.ds(pl.multiple_of(t * BLK, BLK), BLK)
        for h in range(GROUP):
            scaled = q_ref[h, q_rows, :].astype(jnp.float32) * scale
            high = scaled.astype(jnp.bfloat16)
            qs_ref[h * BLK : (h + 1) * BLK, 0:HD] = high
            qs_ref[h * BLK : (h + 1) * BLK, HD:] = (scaled - high.astype(jnp.float32)).astype(jnp.bfloat16)
        m_ref[...] = jnp.full_like(m_ref, MINUS)
        l_ref[...] = jnp.zeros_like(l_ref)
        acc_ref[...] = jnp.zeros_like(acc_ref)

        def step(begin, size, masked):
            key_list, value_list = [], []
            for j in range(size):
                key_at = pl.multiple_of(table_ref[begin + j] * BLK, BLK)
                value_at = pl.multiple_of(table_ref[LIST + begin + j] * BLK, BLK)
                key_list.append(kv_ref[pl.ds(key_at, BLK), :])
                value_list.append(kv_ref[pl.ds(value_at + half, BLK), :])
            key_tile = jnp.concatenate(key_list, axis=0)
            value_tile = jnp.concatenate(value_list, axis=0)
            twice = jnp.concatenate([key_tile, key_tile], axis=1)
            s = lax.dot_general(
                qs_ref[...], twice, (((1,), (1,)), ((), ())), preferred_element_type=jnp.float32
            )
            if masked:
                lane = lax.broadcasted_iota(jnp.int32, (rows, BLK), 1)
                row = lax.broadcasted_iota(jnp.int32, (rows, BLK), 0) & (BLK - 1)
                most = jnp.where(kind == 1, last - 1, block * BLK + row) - lane
                s = jnp.concatenate(
                    [
                        jnp.where(
                            table_ref[2 * LIST + begin + j] * BLK <= most, s[:, j * BLK : (j + 1) * BLK], MINUS
                        )
                        for j in range(size)
                    ],
                    axis=1,
                )
            m_old = m_ref[...]
            m_new = jnp.maximum(m_old, jnp.max(s, axis=1, keepdims=True))
            p = jnp.exp2(s - jnp.concatenate([m_new] * size, axis=1))
            fade = jnp.exp2(m_old - m_new)
            l_ref[...] = l_ref[...] * fade + sum(p[:, i * BLK : (i + 1) * BLK] for i in range(size))
            m_ref[...] = m_new
            acc_ref[...] = acc_ref[...] * fade + jnp.dot(
                p.astype(jnp.bfloat16), value_tile, preferred_element_type=jnp.float32
            )

        full = lax.div(jnp.maximum(count - 1, 0), CHUNK)

        def full_step(chunk, _):
            step(chunk * CHUNK, CHUNK, False)
            return 0

        lax.fori_loop(0, full, full_step, 0)
        rest = count - full * CHUNK
        for size in (4, 8, 16):

            @pl.when((rest > (8 if size == 16 else size - 4)) & (rest <= size))
            def _(size=size):
                step(full * CHUNK, size, True)

        lane = lax.broadcasted_iota(jnp.int32, (BLK, BLK), 1)
        stats = jnp.zeros((BLK, BLK), jnp.float32)
        for h in range(GROUP):
            part = slice(h * BLK, (h + 1) * BLK)
            total = jnp.sum(l_ref[part, :], axis=1, keepdims=True)
            safe = jnp.where(total > 0, total, 1.0)
            out_ref[q_rows, h * HD : (h + 1) * HD] = (acc_ref[part, :] / safe).astype(jnp.bfloat16)
            level = m_ref[part, :] + jnp.log2(safe)
            high = level.astype(jnp.bfloat16).astype(jnp.float32)
            middle = (level - high).astype(jnp.bfloat16).astype(jnp.float32)
            stats = jnp.where(lane == h, high, stats)
            stats = jnp.where(lane == 8 + h, middle, stats)
            stats = jnp.where(lane == 16 + h, level - high - middle, stats)
        out_ref[q_rows, FEATS:] = stats.astype(jnp.bfloat16)
        return 0

    def send_block(t, _):
        one_block(t, 0)
        for i in range(2):

            @pl.when(t == i)
            def _(i=i):
                out_copies[i].start()

        return 0

    lax.fori_loop(0, 2, send_block, 0)
    for copy in out_copies:
        copy.wait()


def attend(side, table, q, parts):
    part_rows = parts[0].shape[0]
    rows = GROUP * BLK
    return pl.pallas_call(
        functools.partial(attend_kernel, side),
        out_shape=(jax.ShapeDtypeStruct((ROWS, FEATS + BLK), jnp.bfloat16),),
        in_specs=[ANYWHERE] * 10,
        out_specs=(ANYWHERE,),
        scratch_shapes=[
            pltpu.SMEM((TABLE,), jnp.int32),
            pltpu.VMEM(q.shape, jnp.bfloat16),
            pltpu.VMEM((ROWS, FEATS + BLK), jnp.bfloat16),
            pltpu.VMEM((8 * part_rows, HD), jnp.bfloat16),
            pltpu.VMEM((rows, 2 * HD), jnp.bfloat16),
            pltpu.VMEM((rows, BLK), jnp.float32),
            pltpu.VMEM((rows, BLK), jnp.float32),
            pltpu.VMEM((rows, HD), jnp.float32),
            pltpu.SemaphoreType.DMA((8,)),
            pltpu.SemaphoreType.DMA((2,)),
            pltpu.SemaphoreType.DMA((2,)),
        ],
        compiler_params=pltpu.CompilerParams(vmem_limit_bytes=32 * 1024 * 1024),
        cost_estimate=pl.CostEstimate(flops=4_000_000_000, bytes_accessed=3_000_000, transcendentals=4_000_000),
        name="attend",
    )(table, q, *parts)


def project_kernel(table_hbm, a_hbm, b_hbm, w_ref, keep_ref, send_ref, table_ref, a_ref, b_ref, att_ref, in_sem):
    tile = w_ref.shape[1] // W_TILES
    in_copies = [
        pltpu.make_async_copy(source, target, in_sem.at[i])
        for i, (source, target) in enumerate(((table_hbm, table_ref), (a_hbm, a_ref), (b_hbm, b_ref)))
    ]
    for copy in in_copies:
        copy.start()
    for copy in in_copies:
        copy.wait()
    my_zh, my_core = table_ref[HEAD_AT], table_ref[HEAD_AT + 1]
    stats_a = a_ref[:, FEATS:].astype(jnp.float32)
    stats_b = b_ref[:, FEATS:].astype(jnp.float32)
    gap = stats_b - stats_a
    for h in range(GROUP):
        levels = gap[:, h : h + 1] + gap[:, 8 + h : 9 + h] + gap[:, 16 + h : 17 + h]
        weight_a = 1.0 / (1.0 + jnp.exp2(jnp.broadcast_to(levels, (ROWS, HD))))
        cols = slice(h * HD, (h + 1) * HD)
        a, b = a_ref[:, cols].astype(jnp.float32), b_ref[:, cols].astype(jnp.float32)
        att_ref[:, cols] = (b + (a - b) * weight_a).astype(jnp.bfloat16)
    for i in range(W_TILES):
        cols = slice(i * tile, (i + 1) * tile)
        res = jnp.dot(att_ref[...], w_ref[:, cols], preferred_element_type=jnp.float32).astype(jnp.bfloat16)
        for z in range(4):
            to = (z - my_zh) & 3
            zero, one = res[z * 64 : z * 64 + 32, :], res[z * 64 + 32 : z * 64 + 64, :]
            keep_ref[to, :, cols] = jnp.where(my_core == 0, zero, one)
            send_ref[to, :, cols] = jnp.where(my_core == 0, one, zero)


def project(table, a, b, w):
    piece = jax.ShapeDtypeStruct((4, 32, w.shape[1]), jnp.bfloat16)
    return pl.pallas_call(
        project_kernel,
        out_shape=(piece, piece),
        in_specs=[ANYWHERE] * 3 + [VMEM],
        out_specs=(VMEM, VMEM),
        scratch_shapes=[
            pltpu.SMEM((TABLE,), jnp.int32),
            pltpu.VMEM(a.shape, jnp.bfloat16),
            pltpu.VMEM(b.shape, jnp.bfloat16),
            pltpu.VMEM((ROWS, FEATS), jnp.bfloat16),
            pltpu.SemaphoreType.DMA((3,)),
        ],
        compiler_params=pltpu.CompilerParams(vmem_limit_bytes=20 * 1024 * 1024),
        cost_estimate=pl.CostEstimate(flops=1_640_000_000, bytes_accessed=9_000_000, transcendentals=1792),
        name="project",
    )(table, a, b, w)


def body(queries, keys, values, out_weight, segment_info, block_order):
    k, v = keys[:, 0, :], values[:, 0, :]
    q = jnp.transpose(queries, (1, 0, 2))
    other_q = shift(q, "zl", 1)
    k = [k] + [shift(k, "y", o) for o in OFFSETS[1:]]
    v = [v] + [shift(v, "x", o) for o in OFFSETS[1:]]
    table = jnp.minimum(make_table(block_order, segment_info.T), 1 << 20)
    k, other_q = lax.optimization_barrier((k, other_q))
    k = jnp.concatenate(k, axis=0)
    v = jnp.concatenate(v, axis=0)
    parts = [k, v]
    for o in OFFSETS[1:]:
        parts += lax.optimization_barrier((shift(v, "y", o), shift(k, "x", o)))
    (other,) = attend(0, table, other_q, parts)
    back = shift(other, "zl", 1)
    (own,) = attend(1, table, q, parts)
    keep, send = project(table, own, back, out_weight)
    pieces = keep.astype(jnp.float32) + shift(send, "core", 1).astype(jnp.float32)
    low = pieces.astype(jnp.bfloat16)
    top, bottom = slice(0, 16), slice(16, 32)
    from_behind, from_ahead = lax.optimization_barrier((shift(low[2, top], "zh", -1), shift(low[2, bottom], "zh", 1)))
    ahead = (pieces[1, top] + from_behind.astype(jnp.float32)).astype(jnp.bfloat16)
    back = (pieces[3, bottom] + from_ahead.astype(jnp.float32)).astype(jnp.bfloat16)
    behind = [shift(ahead, "zh", -1), shift(low[1, bottom], "zh", -1)]
    beyond = [shift(low[3, top], "zh", 1), shift(back, "zh", 1)]
    behind, beyond = jnp.concatenate(behind, axis=0), jnp.concatenate(beyond, axis=0)
    total = pieces[0] + behind.astype(jnp.float32) + beyond.astype(jnp.float32)
    return total.astype(jnp.bfloat16)


def solution(mesh):
    fine = Mesh(mesh.devices.reshape(tuple(SIZES.values())), AXES)
    placed = (
        P(CTX, HEAD, None),
        P(CTX, HEAD, None),
        P(CTX, HEAD, None),
        P(HEAD, None),
        P(),
        P(),
    )
    return jax.shard_map(body, mesh=fine, in_specs=placed, out_specs=P(AXES, None), check_vma=False)
```

```python
import functools
import math

import jax
import jax.numpy as jnp
from jax import lax
from jax.experimental import pallas as pl
from jax.experimental.pallas import tpu as pltpu
from jax.sharding import Mesh, PartitionSpec as P

BLK = 128
HD = 128
GROUP = 7
ROWS = 256
FEATS = GROUP * HD
BLOCKS = 64
CHUNK = 16
LIST = 48
QUERY_AT = 3 * LIST
HEAD_AT = QUERY_AT + 16
TABLE = 256
W_TILES = 2
MINUS = -1e30
SIZES = {"x": 4, "zl": 2, "y": 4, "zh": 4, "core": 2}
AXES = tuple(SIZES)
CTX = ("x", "zl", "y")
HEAD = ("zh", "core")
OFFSETS = (0, 1, -1, 2)
PLACES = (0, 4, 5, 1, 6, 2, 7, 3)
SMEM = pl.BlockSpec(memory_space=pltpu.SMEM)
VMEM = pl.BlockSpec(memory_space=pltpu.VMEM)
ANYWHERE = pl.BlockSpec(memory_space=pl.ANY)


def shift(value, axis, step):
    size = SIZES[axis]
    return lax.ppermute(value, axis, [((i + step) % size, i) for i in range(size)])


def table_kernel(order_ref, info_ref, out_ref, table_ref, inv_ref, sem):
    my_x, my_zl, my_y = (lax.axis_index(axis) for axis in CTX)

    def invert(block, _):
        inv_ref[order_ref[block]] = block
        return 0

    lax.fori_loop(0, BLOCKS, invert, 0)
    table_ref[HEAD_AT] = lax.axis_index("zh")
    table_ref[HEAD_AT + 1] = lax.axis_index("core")
    ends = []
    for i in range(4):
        pair_zl = my_zl ^ 1 if i < 2 else my_zl
        block = order_ref[((my_x * 2 + pair_zl) * 4 + my_y) * 2 + i % 2]
        last, kind = info_ref[1, block], info_ref[2, block]
        at = QUERY_AT + 4 * i
        table_ref[at], table_ref[at + 1], table_ref[at + 2] = block, kind, last
        ends.append(jnp.where(kind == 1, lax.div(last, BLK) - 1, block))

    def place(position, carry):
        count, seen = carry[0], carry[1:]
        block = inv_ref[position]
        ctx = block >> 1
        x_off, y_off = ((ctx >> 3) - my_x) & 3, ((ctx & 3) - my_y) & 3
        x_part, y_part = (x_off ^ (x_off >> 1)), (y_off ^ (y_off >> 1))
        here = ((ctx >> 2) & 1) == my_zl
        table_ref[count] = (x_part * 4 + y_part) * 2 + (block & 1)
        table_ref[LIST + count] = (y_part * 4 + x_part) * 2 + (block & 1)
        table_ref[2 * LIST + count] = position
        count = count + here.astype(jnp.int32)
        return (count,) + tuple(jnp.where(position == end, count, s) for end, s in zip(ends, seen))

    done = lax.fori_loop(0, BLOCKS, place, (jnp.int32(0),) * 5)
    for i in range(4):
        table_ref[QUERY_AT + 4 * i + 3] = done[1 + i]
    for i in range(BLOCKS // 2, LIST):
        table_ref[i] = 0
        table_ref[LIST + i] = 0
        table_ref[2 * LIST + i] = BLOCKS
    copy = pltpu.make_async_copy(table_ref, out_ref, sem)
    copy.start()
    copy.wait()


def make_table(order, info):
    return pl.pallas_call(
        table_kernel,
        out_shape=jax.ShapeDtypeStruct((TABLE,), jnp.int32),
        in_specs=[SMEM, SMEM],
        out_specs=ANYWHERE,
        scratch_shapes=[
            pltpu.SMEM((TABLE,), jnp.int32),
            pltpu.SMEM((BLOCKS,), jnp.int32),
            pltpu.SemaphoreType.DMA,
        ],
        cost_estimate=pl.CostEstimate(flops=2_000_000_000, bytes_accessed=1000, transcendentals=0),
        name="table",
    )(order, info)


def attend_kernel(side, table_hbm, q_hbm, *refs):
    parts, refs = refs[:8], refs[8:]
    out_hbm, *refs = refs
    table_ref, q_ref, out_ref, kv_ref, qs_ref, m_ref, l_ref, acc_ref, kv_sem, in_sem, out_sem = refs
    part_rows = parts[0].shape[0]
    half = 4 * part_rows
    table_copy = pltpu.make_async_copy(table_hbm, table_ref, in_sem.at[0])
    q_copy = pltpu.make_async_copy(q_hbm, q_ref, in_sem.at[1])
    copies = [
        pltpu.make_async_copy(part, kv_ref.at[pl.ds(i * part_rows, part_rows)], kv_sem.at[i])
        for i, part in zip(PLACES, parts)
    ]
    out_copies = [
        pltpu.make_async_copy(
            out_ref.at[pl.ds(t * BLK, BLK)], out_hbm.at[pl.ds(t * BLK, BLK)], out_sem.at[t]
        )
        for t in range(2)
    ]
    table_copy.start()
    q_copy.start()
    for copy in copies:
        copy.start()
    scale = math.log2(math.e) / math.sqrt(HD)
    rows = GROUP * BLK
    q_copy.wait()
    for h in range(GROUP):
        scaled = q_ref[h].astype(jnp.float32) * scale
        high = scaled.astype(jnp.bfloat16)
        low = (scaled - high.astype(jnp.float32)).astype(jnp.bfloat16)
        for t in range(2):
            into, part = slice(t * rows + h * BLK, t * rows + (h + 1) * BLK), slice(t * BLK, (t + 1) * BLK)
            qs_ref[into, 0:HD] = high[part]
            qs_ref[into, HD:] = low[part]
    table_copy.wait()
    for copy in copies:
        copy.wait()

    def one_block(t, _):
        at = QUERY_AT + 4 * (2 * side + t)
        block, kind, last, count = table_ref[at], table_ref[at + 1], table_ref[at + 2], table_ref[at + 3]
        q_rows = pl.ds(pl.multiple_of(t * BLK, BLK), BLK)
        q_at = pl.multiple_of(t * rows, rows)
        m_ref[...] = jnp.full_like(m_ref, MINUS)
        l_ref[...] = jnp.zeros_like(l_ref)
        acc_ref[...] = jnp.zeros_like(acc_ref)

        def step(begin, size, masked):
            key_list, value_list = [], []
            for j in range(size):
                key_at = pl.multiple_of(table_ref[begin + j] * BLK, BLK)
                value_at = pl.multiple_of(table_ref[LIST + begin + j] * BLK, BLK)
                key_list.append(kv_ref[pl.ds(key_at, BLK), :])
                value_list.append(kv_ref[pl.ds(value_at + half, BLK), :])
            key_tile = jnp.concatenate(key_list, axis=0)
            value_tile = jnp.concatenate(value_list, axis=0)
            twice = jnp.concatenate([key_tile, key_tile], axis=1)
            s = lax.dot_general(
                qs_ref[pl.ds(q_at, rows), :], twice, (((1,), (1,)), ((), ())), preferred_element_type=jnp.float32
            )
            if masked:
                lane = lax.broadcasted_iota(jnp.int32, (rows, BLK), 1)
                row = lax.broadcasted_iota(jnp.int32, (rows, BLK), 0) & (BLK - 1)
                most = jnp.where(kind == 1, last - 1, block * BLK + row) - lane
                s = jnp.concatenate(
                    [
                        s[:, j * BLK : (j + 1) * BLK]
                        if j < size - (8 if size == 16 else 4)
                        else jnp.where(
                            table_ref[2 * LIST + begin + j] * BLK <= most, s[:, j * BLK : (j + 1) * BLK], MINUS
                        )
                        for j in range(size)
                    ],
                    axis=1,
                )
            m_old = m_ref[...]
            m_new = jnp.maximum(m_old, jnp.max(s, axis=1, keepdims=True))
            p = jnp.exp2(s - jnp.concatenate([m_new] * size, axis=1))
            fade = jnp.exp2(m_old - m_new)
            l_ref[...] = l_ref[...] * fade + sum(p[:, i * BLK : (i + 1) * BLK] for i in range(size))
            m_ref[...] = m_new
            acc_ref[...] = acc_ref[...] * fade + jnp.dot(
                p.astype(jnp.bfloat16), value_tile, preferred_element_type=jnp.float32
            )

        full = lax.div(jnp.maximum(count - 1, 0), CHUNK)

        def full_step(chunk, _):
            step(chunk * CHUNK, CHUNK, False)
            return 0

        lax.fori_loop(0, full, full_step, 0)
        rest = count - full * CHUNK
        for size in (4, 8, 16):

            @pl.when((rest > (8 if size == 16 else size - 4)) & (rest <= size))
            def _(size=size):
                step(full * CHUNK, size, True)

        lane = lax.broadcasted_iota(jnp.int32, (BLK, BLK), 1)
        stats = jnp.zeros((BLK, BLK), jnp.float32)
        for h in range(GROUP):
            part = slice(h * BLK, (h + 1) * BLK)
            total = jnp.sum(l_ref[part, :], axis=1, keepdims=True)
            safe = jnp.where(total > 0, total, 1.0)
            out_ref[q_rows, h * HD : (h + 1) * HD] = (acc_ref[part, :] / safe).astype(jnp.bfloat16)
            level = m_ref[part, :] + jnp.log2(safe)
            high = level.astype(jnp.bfloat16).astype(jnp.float32)
            middle = (level - high).astype(jnp.bfloat16).astype(jnp.float32)
            stats = jnp.where(lane == h, high, stats)
            stats = jnp.where(lane == 8 + h, middle, stats)
            stats = jnp.where(lane == 16 + h, level - high - middle, stats)
        out_ref[q_rows, FEATS:] = stats.astype(jnp.bfloat16)
        return 0

    def send_block(t, _):
        one_block(t, 0)
        for i in range(2):

            @pl.when(t == i)
            def _(i=i):
                out_copies[i].start()

        return 0

    lax.fori_loop(0, 2, send_block, 0)
    for copy in out_copies:
        copy.wait()


def attend(side, table, q, parts):
    part_rows = parts[0].shape[0]
    rows = GROUP * BLK
    return pl.pallas_call(
        functools.partial(attend_kernel, side),
        out_shape=(jax.ShapeDtypeStruct((ROWS, FEATS + BLK), jnp.bfloat16),),
        in_specs=[ANYWHERE] * 10,
        out_specs=(ANYWHERE,),
        scratch_shapes=[
            pltpu.SMEM((TABLE,), jnp.int32),
            pltpu.VMEM(q.shape, jnp.bfloat16),
            pltpu.VMEM((ROWS, FEATS + BLK), jnp.bfloat16),
            pltpu.VMEM((8 * part_rows, HD), jnp.bfloat16),
            pltpu.VMEM((2 * rows, 2 * HD), jnp.bfloat16),
            pltpu.VMEM((rows, BLK), jnp.float32),
            pltpu.VMEM((rows, BLK), jnp.float32),
            pltpu.VMEM((rows, HD), jnp.float32),
            pltpu.SemaphoreType.DMA((8,)),
            pltpu.SemaphoreType.DMA((2,)),
            pltpu.SemaphoreType.DMA((2,)),
        ],
        compiler_params=pltpu.CompilerParams(vmem_limit_bytes=32 * 1024 * 1024),
        cost_estimate=pl.CostEstimate(flops=4_000_000_000, bytes_accessed=3_000_000, transcendentals=4_000_000),
        name="attend",
    )(table, q, *parts)


def project_kernel(table_hbm, a_hbm, b_hbm, w_ref, keep_ref, send_ref, table_ref, a_ref, b_ref, att_ref, in_sem):
    tile = w_ref.shape[1] // W_TILES
    in_copies = [
        pltpu.make_async_copy(source, target, in_sem.at[i])
        for i, (source, target) in enumerate(((table_hbm, table_ref), (a_hbm, a_ref), (b_hbm, b_ref)))
    ]
    for copy in in_copies:
        copy.start()
    for copy in in_copies:
        copy.wait()
    my_zh, my_core = table_ref[HEAD_AT], table_ref[HEAD_AT + 1]
    stats_a = a_ref[:, FEATS:].astype(jnp.float32)
    stats_b = b_ref[:, FEATS:].astype(jnp.float32)
    gap = stats_b - stats_a
    for h in range(GROUP):
        levels = gap[:, h : h + 1] + gap[:, 8 + h : 9 + h] + gap[:, 16 + h : 17 + h]
        weight_a = 1.0 / (1.0 + jnp.exp2(jnp.broadcast_to(levels, (ROWS, HD))))
        cols = slice(h * HD, (h + 1) * HD)
        a, b = a_ref[:, cols].astype(jnp.float32), b_ref[:, cols].astype(jnp.float32)
        att_ref[:, cols] = (b + (a - b) * weight_a).astype(jnp.bfloat16)
    for i in range(W_TILES):
        cols = slice(i * tile, (i + 1) * tile)
        res = jnp.dot(att_ref[...], w_ref[:, cols], preferred_element_type=jnp.float32).astype(jnp.bfloat16)
        for z in range(4):
            to = (z - my_zh) & 3
            zero, one = res[z * 64 : z * 64 + 32, :], res[z * 64 + 32 : z * 64 + 64, :]
            keep_ref[to, :, cols] = jnp.where(my_core == 0, zero, one)
            send_ref[to, :, cols] = jnp.where(my_core == 0, one, zero)


def project(table, a, b, w):
    piece = jax.ShapeDtypeStruct((4, 32, w.shape[1]), jnp.bfloat16)
    return pl.pallas_call(
        project_kernel,
        out_shape=(piece, piece),
        in_specs=[ANYWHERE] * 3 + [VMEM],
        out_specs=(VMEM, VMEM),
        scratch_shapes=[
            pltpu.SMEM((TABLE,), jnp.int32),
            pltpu.VMEM(a.shape, jnp.bfloat16),
            pltpu.VMEM(b.shape, jnp.bfloat16),
            pltpu.VMEM((ROWS, FEATS), jnp.bfloat16),
            pltpu.SemaphoreType.DMA((3,)),
        ],
        compiler_params=pltpu.CompilerParams(vmem_limit_bytes=20 * 1024 * 1024),
        cost_estimate=pl.CostEstimate(flops=1_640_000_000, bytes_accessed=9_000_000, transcendentals=1792),
        name="project",
    )(table, a, b, w)


def body(queries, keys, values, out_weight, segment_info, block_order):
    k, v = keys[:, 0, :], values[:, 0, :]
    q = jnp.transpose(queries, (1, 0, 2))
    other_q = shift(q, "zl", 1)
    k = [k] + [shift(k, "y", o) for o in OFFSETS[1:]]
    v = [v] + [shift(v, "x", o) for o in OFFSETS[1:]]
    table = jnp.minimum(make_table(block_order, segment_info.T), 1 << 20)
    k, other_q = lax.optimization_barrier((k, other_q))
    k = jnp.concatenate(k, axis=0)
    v = jnp.concatenate(v, axis=0)
    parts = [k, v]
    for o in OFFSETS[1:]:
        parts += lax.optimization_barrier((shift(v, "y", o), shift(k, "x", o)))
    (other,) = attend(0, table, other_q, parts)
    back = shift(other, "zl", 1)
    (own,) = attend(1, table, q, parts)
    keep, send = project(table, own, back, out_weight)
    pieces = keep.astype(jnp.float32) + shift(send, "core", 1).astype(jnp.float32)
    low = pieces.astype(jnp.bfloat16)
    top, bottom = slice(0, 16), slice(16, 32)
    from_behind, from_ahead = lax.optimization_barrier((shift(low[2, top], "zh", -1), shift(low[2, bottom], "zh", 1)))
    ahead = (pieces[1, top] + from_behind.astype(jnp.float32)).astype(jnp.bfloat16)
    back = (pieces[3, bottom] + from_ahead.astype(jnp.float32)).astype(jnp.bfloat16)
    behind = [shift(ahead, "zh", -1), shift(low[1, bottom], "zh", -1)]
    beyond = [shift(low[3, top], "zh", 1), shift(back, "zh", 1)]
    behind, beyond = jnp.concatenate(behind, axis=0), jnp.concatenate(beyond, axis=0)
    total = pieces[0] + behind.astype(jnp.float32) + beyond.astype(jnp.float32)
    return total.astype(jnp.bfloat16)


def solution(mesh):
    fine = Mesh(mesh.devices.reshape(tuple(SIZES.values())), AXES)
    placed = (
        P(CTX, HEAD, None),
        P(CTX, HEAD, None),
        P(CTX, HEAD, None),
        P(HEAD, None),
        P(),
        P(),
    )
    return jax.shard_map(body, mesh=fine, in_specs=placed, out_specs=P(AXES, None), check_vma=False)
```
